128 devices in a mesh: ab: 32 (over x, z, y_lo), cd: 4 (over y_hi, core).
Axes of the slice: x: 4, y: 4 (y_hi: 2, y_lo: 2; y = y_hi * 2 + y_lo), z: 4, core: 2. Of those that a mesh axis runs over, the one named last changes fastest.
Arguments:
- integrals: bfloat16 [96, 96, 128, 512], P('ab', None, None, 'cd'), may hold values from -0.0234375 to 0.0234375
- amplitudes: bfloat16 [16, 512, 512], P(None, 'ab', 'cd'), may hold values from -6 to 6
- block_sizes: int32 [4], replicated, may hold values from 1 to 128, 500 in all
Outputs:
- symmetric_residual: float32 [16, 96, 96], P(None, 'ab')
The draws below stay inside these ranges and needn't reach their ends.
Inputs may be any that keep to these rules, and one draw needn't show every extreme that they name: `block_sizes`: the sizes sum to 500 and the largest is exactly 128.
All inputs are finite; a program needn't handle non-finite values.
Results may differ from the reference program's by a relative error of at most 0.0003.
Values may be sent and summed in bfloat16 or wider, within the bound.
A program may use at most 64 MiB of HBM per device.

```python
import math
import jax
import jax.numpy as jnp
import numpy as np
from jax import lax

IRREPS = 4
BLK = 128
NPAIR = 16
WIN = 96
WIR = 24


def block_levels(rng, extent, shards, least, top_value):
    def one(axis_at, blocks):
        draws = jax.random.uniform(jax.random.fold_in(jax.random.fold_in(rng, 6), axis_at), (blocks,), jnp.float32, least / len(shards), top_value / len(shards))
        return jnp.repeat(jnp.exp(draws), extent[axis_at] // blocks).reshape((-1,) + (1,) * (len(extent) - axis_at - 1))

    factor_of = one(*shards[0])
    for cut in shards[1:]:
        factor_of = factor_of * one(*cut)
    return factor_of


def split_up(amount, total, limit, skew):
    weights = [(1 << 20) // math.isqrt(standing ** skew) + 1 for standing in range(2, amount + 1)]
    surplus, given = total - limit - (amount - 1), [1] * (amount - 1)
    while surplus > 0:
        free = [i for i in range(amount - 1) if given[i] < limit]
        mass, left = sum([weights[i] for i in free]), surplus
        for i in free:
            extra = min(limit - given[i], max(1, left * weights[i] // mass), surplus)
            given[i] = given[i] + extra
            surplus = surplus - extra
    return np.array([limit] + given)


def ragged_sizes(own_key, count, total, most, lean):
    if count == 2:
        one = jax.random.randint(own_key, (), max(1, total - most), min(most, total - 1) + 1)
        return jnp.stack([one, total - one])
    lengths = jnp.asarray(split_up(count, total, most, lean), jnp.int32)
    twos = (count - 1) // 2
    giver, taker = lengths[1:1 + 2 * twos:2], lengths[2:2 + 2 * twos:2]
    margin = jnp.minimum(giver - 1, most - taker)
    passed = jax.random.randint(jax.random.fold_in(own_key, 1), (twos,), 0, 1 << 20) % (margin + 1)
    lengths = lengths.at[1:1 + 2 * twos:2].set(giver - passed).at[2:2 + 2 * twos:2].set(taker + passed)
    return lengths[jax.random.permutation(jax.random.fold_in(own_key, 2), count)]


def normal_values(key, shape, spread, most, cuts=(), held_as=jnp.bfloat16):
    factor_of = block_levels(key, shape, cuts, -0.22, 0.18) if cuts else 1.0
    values = jax.random.normal(key, shape, jnp.float32) * spread * factor_of
    return jnp.minimum(jnp.maximum(values, -most), most).astype(held_as)


def setup_inputs(seed: int = 0) -> dict:
    key_of = jax.random.split(jax.random.key(seed), 4)
    integrals = normal_values(key_of[0], (WIN, WIN, BLK, IRREPS * BLK), (IRREPS * BLK * BLK) ** -0.5, 0.0234375, ((0, 32), (3, 4)))
    amplitudes = normal_values(key_of[1], (NPAIR, IRREPS * BLK, IRREPS * BLK), 1.0, 6.0, ((1, 32), (2, 4)))
    block_sizes = ragged_sizes(key_of[2], IRREPS, IRREPS * BLK - 12, BLK, 2).astype(jnp.int32)
    return dict(integrals=integrals, amplitudes=amplitudes, block_sizes=block_sizes)


def masked_amplitudes(amplitudes, block_sizes):
    slot_ids = jnp.arange(BLK, dtype=jnp.int32)
    valid_slots = (slot_ids[None, :] < block_sizes[:, None]).reshape(IRREPS * BLK)
    keep_mask = valid_slots[:, None] & valid_slots[None, :]
    return jnp.where(keep_mask[None], amplitudes, jnp.zeros_like(amplitudes))


def reference(integrals, amplitudes, block_sizes):
    masked = masked_amplitudes(amplitudes, block_sizes).astype(jnp.float32)
    masked = masked.reshape(NPAIR, IRREPS, BLK, IRREPS, BLK)

    def one_row(row_index):
        row_values = integrals[row_index]
        first_irrep = row_index // WIR
        pieces = []
        for second in range(IRREPS):
            row_block = row_values[second * WIR:(second + 1) * WIR].astype(jnp.float32)
            accumulated = jnp.zeros((NPAIR, WIR), jnp.float32)
            for target in range(IRREPS):
                source = jnp.bitwise_xor(jnp.bitwise_xor(first_irrep, second), target)
                amp_block = lax.dynamic_index_in_dim(masked, source, 1, keepdims=False)[:, :, target, :]
                part_block = row_block[:, :, target * BLK:(target + 1) * BLK]
                accumulated = accumulated + jnp.einsum("bcd,pcd->pb", part_block, amp_block)
            pieces.append(accumulated)
        return jnp.concatenate(pieces, axis=1)

    ladder = lax.map(one_row, jnp.arange(WIN, dtype=jnp.int32))
    ladder = jnp.transpose(ladder, (1, 0, 2))
    return ladder + jnp.transpose(ladder, (0, 2, 1))
```

```python
import jax
import jax.numpy as jnp
from jax import lax
from jax.experimental import pallas as pl
from jax.experimental.pallas import tpu as pltpu
from jax.sharding import PartitionSpec as P

IRREPS = 4
BLK = 128
NPAIR = 16
WIR = 24
GROUP = 8
OWN = 3
CB = 16
MESH = pl.DeviceIdType.MESH
F32 = jnp.float32
BF16 = jnp.bfloat16


def iota(shape, dim):
    return lax.broadcasted_iota(jnp.int32, shape, dim)


def split3(x, axis):
    high = x.astype(BF16)
    rest = x - high.astype(F32)
    middle = rest.astype(BF16)
    low = (rest - middle.astype(F32)).astype(BF16)
    return jnp.concatenate([high, middle, low], axis=axis)


def kernel(
    sizes, amps, integrals, out, ints, panels, acc, own, msgs, mirror, shares,
    ints_sem, amp_send, amp_recv, msg_send, msg_recv, share_send, share_recv,
):
    ab = lax.axis_index("ab")
    cd = lax.axis_index("cd")
    irrep = ab // GROUP
    slot = lax.rem(ab, GROUP)
    slot_low = lax.rem(slot // 2, 2)
    slot_lane = lax.rem(slot, 2)

    fetch = pltpu.make_async_copy(integrals, ints, ints_sem)
    fetch.start()

    barrier = pltpu.get_barrier_semaphore()

    def greet(i, carry):
        pl.semaphore_signal(
            barrier, inc=1, device_id=(lax.rem(ab + i, 32), cd), device_id_type=MESH
        )
        return carry

    lax.fori_loop(1, 32, greet, 0)
    for i in range(1, 4):
        pl.semaphore_signal(barrier, inc=1, device_id=(ab, lax.rem(cd + i, 4)), device_id_type=MESH)

    row_limit = sizes[irrep] - slot * CB
    col_limit = sizes[cd]
    shape = (NPAIR * CB, BLK)
    keep = (lax.rem(iota(shape, 0), CB) < row_limit) & (iota(shape, 1) < col_limit)
    plain = amps[...].reshape(shape).astype(F32)
    panels[ab] = jnp.where(keep, plain, 0.0).T.astype(BF16)

    pl.semaphore_wait(barrier, 34)

    def amp_copy(i, peer, block):
        return pltpu.make_async_remote_copy(
            src_ref=panels.at[block],
            dst_ref=panels.at[block],
            send_sem=amp_send.at[i],
            recv_sem=amp_recv.at[block],
            device_id=(peer, cd),
            device_id_type=MESH,
        )

    def spread(i, carry):
        amp_copy(i, ab ^ i, ab).start()
        return carry

    lax.fori_loop(1, 32, spread, 0)
    fetch.wait()

    low_half = lax.rem(iota((8, 256), 1), 16) < 8
    diagonal = lax.rem(iota((8, 256), 1), 8) == iota((8, 256), 0)
    spread_pairs = (
        lax.rem(iota((768, 128), 1), 16) == lax.rem(iota((768, 128), 0), 256) // CB
    ).astype(BF16)
    row = iota((72, 128), 0)
    lane = iota((72, 128), 1)
    lane_slot, lane_item = lane // 64, lax.rem(lane, 64) // 16
    row_a, row_b = row // WIR, lax.rem(row, WIR)
    own_keep = (lane_slot == lax.rem(row_b // OWN, 2)) & (lane_item == lax.rem(row_b, OWN))
    msg_keep = (lane_slot == slot_lane) & (lane_item == row_a)
    to = iota((80, 144), 0)
    frm = iota((80, 144), 1)
    frm_row = lax.rem(frm, 72)
    frm_a, frm_b = frm_row // WIR, lax.rem(frm_row, WIR)
    frm_slot, frm_k = frm_b // OWN, lax.rem(frm_b, OWN)
    place = jnp.where(
        frm < 72,
        (frm_slot // 4) * 8 + lax.rem(frm_slot // 2, 2) * 4 + frm_a,
        16 + frm_slot * 8 + slot_low * 4 + frm_k,
    )
    gather_rows = (to == place).astype(BF16)
    gather_rows = jnp.concatenate([gather_rows] * 3, axis=1)

    def msg_copy(peer, block, sender):
        return pltpu.make_async_remote_copy(
            src_ref=msgs.at[block],
            dst_ref=mirror.at[sender],
            send_sem=msg_send.at[block],
            recv_sem=msg_recv.at[sender],
            device_id=(peer, cd),
            device_id_type=MESH,
        )

    def panel(step, carry):
        rel = step ^ (step // 2)
        source = irrep ^ rel
        second = source ^ irrep ^ cd

        def pair(t, inner):
            for j in range(2):
                block = source * GROUP + 2 * t + j

                @pl.when(block != ab)
                def _():
                    amp_copy(0, ab, block).wait_recv()

            first_block = source * GROUP + 2 * t
            weights = panels[pl.ds(first_block, 2)].reshape(256, 256)
            first_c = pl.multiple_of(2 * t * CB, 2 * CB)
            for a in range(OWN):
                rows = ints[a, pl.ds(second * WIR, WIR), pl.ds(first_c, 2 * CB), :]
                left = jnp.concatenate([rows[:, :CB], rows[:, CB:]], axis=2).reshape(WIR * CB, 256)
                term = jnp.dot(left, weights, preferred_element_type=F32)
                term = term.reshape(WIR, 2, 8, 256)
                term = jnp.where(low_half[None], term[:, 0], term[:, 1])
                here = pl.ds(a * WIR, WIR)
                acc[here] = jnp.where(t == 0, term, acc[here] + term)
            return inner

        lax.fori_loop(0, 4, pair, 0)
        folded = jnp.sum(jnp.where(diagonal[None], acc[...], 0.0), axis=1)
        values = jnp.dot(split3(folded, 1), spread_pairs, preferred_element_type=F32)
        both = jnp.concatenate(
            [jnp.where(own_keep, values, 0.0), jnp.where(msg_keep, values, 0.0)], axis=0
        )
        placed = jnp.dot(gather_rows, split3(both, 0), preferred_element_type=F32)
        own[second] = placed[:16].reshape(2, 8, 128)
        msgs[pl.ds(second * GROUP, GROUP)] = placed[16:].reshape(GROUP, 8, 128)

        def send(i, inner):
            peer = second * GROUP + i

            @pl.when(peer != ab)
            def _():
                msg_copy(peer, peer, ab).start()

            return inner

        lax.fori_loop(0, GROUP, send, 0)
        return carry

    lax.fori_loop(0, IRREPS, panel, 0)
    mirror[ab] = msgs[ab]

    def collect(i, carry):
        msg_copy(ab, ab, ab ^ i).wait_recv()
        return carry

    lax.fori_loop(1, 32, collect, 0)
    total = own[...] + jnp.sum(mirror[...].reshape(IRREPS, 2, 4, 8, 128), axis=2)
    shares[cd] = total

    def share_copy(i, peer, sender):
        return pltpu.make_async_remote_copy(
            src_ref=shares.at[sender],
            dst_ref=shares.at[sender],
            send_sem=share_send.at[i],
            recv_sem=share_recv.at[sender],
            device_id=(ab, peer),
            device_id_type=MESH,
        )

    for i in range(1, 4):
        share_copy(i, cd ^ i, cd).start()
    for i in range(1, 4):
        share_copy(i, cd, cd ^ i).wait_recv()
    out[...] = (shares[0] + shares[1]) + (shares[2] + shares[3])

    def finish(i, carry):
        amp_copy(i, ab, ab).wait_send()
        msg_copy(ab, ab ^ i, ab).wait_send()
        return carry

    lax.fori_loop(1, 32, finish, 0)
    for i in range(1, 4):
        share_copy(i, cd, cd).wait_send()


def on_device(integrals, amplitudes, block_sizes):
    vmem = pl.BlockSpec(memory_space=pltpu.VMEM)
    packed = pl.pallas_call(
        kernel,
        out_shape=jax.ShapeDtypeStruct((IRREPS, 2, 8, 128), F32),
        in_specs=[
            pl.BlockSpec(memory_space=pltpu.SMEM),
            vmem,
            pl.BlockSpec(memory_space=pl.ANY),
        ],
        out_specs=vmem,
        scratch_shapes=[
            pltpu.VMEM(integrals.shape, BF16),
            pltpu.VMEM((32, BLK, NPAIR * CB), BF16),
            pltpu.VMEM((OWN * WIR, 8, 256), F32),
            pltpu.VMEM((IRREPS, 2, 8, 128), F32),
            pltpu.VMEM((32, 8, 128), F32),
            pltpu.VMEM((32, 8, 128), F32),
            pltpu.VMEM((4, IRREPS, 2, 8, 128), F32),
            pltpu.SemaphoreType.DMA,
            pltpu.SemaphoreType.DMA((32,)),
            pltpu.SemaphoreType.DMA((32,)),
            pltpu.SemaphoreType.DMA((32,)),
            pltpu.SemaphoreType.DMA((32,)),
            pltpu.SemaphoreType.DMA((4,)),
            pltpu.SemaphoreType.DMA((4,)),
        ],
        compiler_params=pltpu.CompilerParams(
            collective_id=0, has_side_effects=True, vmem_limit_bytes=56 << 20
        ),
        name="ladder",
    )(block_sizes, amplitudes, integrals)
    packed = packed.reshape(IRREPS, 2, 2, 4, 2, 4, NPAIR)[:, :, :, :OWN, :, :OWN]
    return packed.transpose(6, 3, 0, 1, 2, 4, 5).reshape(NPAIR, OWN, IRREPS * WIR)


def solution(mesh):
    placed = (P("ab", None, None, "cd"), P(None, "ab", "cd"), P())
    return jax.shard_map(
        on_device, mesh=mesh, in_specs=placed, out_specs=P(None, "ab", None), check_vma=False
    )
```

```python
import jax
import jax.numpy as jnp
from jax import lax
from jax.experimental import pallas as pl
from jax.experimental.pallas import tpu as pltpu
from jax.sharding import PartitionSpec as P

IRREPS = 4
BLK = 128
NPAIR = 16
WIR = 24
GROUP = 8
OWN = 3
CB = 16
MESH = pl.DeviceIdType.MESH
F32 = jnp.float32
BF16 = jnp.bfloat16


def iota(shape, dim):
    return lax.broadcasted_iota(jnp.int32, shape, dim)


def split3(x, axis):
    high = x.astype(BF16)
    rest = x - high.astype(F32)
    middle = rest.astype(BF16)
    low = (rest - middle.astype(F32)).astype(BF16)
    return jnp.concatenate([high, middle, low], axis=axis)


def kernel(
    sizes, amps, integrals, out, ints, plain, panels, acc, own, msgs, mirror, shares,
    ints_sem, plain_sem, send_sem, item_recv, pair_recv, msg_send, msg_recv, share_send, share_recv,
):
    ab = lax.axis_index("ab")
    cd = lax.axis_index("cd")
    irrep = ab // GROUP
    slot = lax.rem(ab, GROUP)
    slot_low = lax.rem(slot // 2, 2)
    slot_lane = lax.rem(slot, 2)
    ring = slot // 2
    pick = slot_lane

    fetch_own = pltpu.make_async_copy(amps, plain, plain_sem)
    fetch_own.start()

    def place(half, du, dv, y):
        if half == 0:
            return lax.rem(irrep + dv, 4) * GROUP + lax.rem(ring + du, 4) * 2 + y
        return lax.rem(irrep + du, 4) * GROUP + lax.rem(ring + dv, 4) * 2 + y

    plane = [(0, 1), (1, 0), (3, 0), (1, 1), (3, 1), (2, 0), (2, 1)]

    def peer_of(half, du, dy):
        return place(half, du, 0, lax.rem(pick + dy, 2))

    barrier = pltpu.get_barrier_semaphore()
    for half in range(2):
        for du, dy in plane[half:]:
            pl.semaphore_signal(
                barrier, inc=1, device_id=(peer_of(half, du, dy), cd), device_id_type=MESH
            )
    for i in range(1, 4):
        pl.semaphore_signal(barrier, inc=1, device_id=(ab, cd ^ i), device_id_type=MESH)

    fetch = pltpu.make_async_copy(integrals, ints, ints_sem)
    fetch.start()

    row_limit = sizes[irrep] - slot * CB
    col_limit = sizes[cd]
    shape = (NPAIR * CB, BLK)
    keep = (lax.rem(iota(shape, 0), CB) < row_limit) & (iota(shape, 1) < col_limit)
    fetch_own.wait()
    turned = jnp.where(keep, plain[...].reshape(shape).astype(F32), 0.0).T.astype(BF16)
    panels[0, ab] = turned[:, :128]
    panels[1, ab] = turned[:, 128:]

    def item_copy(i, half, peer, block):
        return pltpu.make_async_remote_copy(
            src_ref=panels.at[half, block],
            dst_ref=panels.at[half, block],
            send_sem=send_sem.at[i],
            recv_sem=item_recv.at[half, block],
            device_id=(peer, cd),
            device_id_type=MESH,
        )

    def pair_copy(i, half, peer, first):
        return pltpu.make_async_remote_copy(
            src_ref=panels.at[half, pl.ds(first, 2)],
            dst_ref=panels.at[half, pl.ds(first, 2)],
            send_sem=send_sem.at[i],
            recv_sem=pair_recv.at[half, first // 2],
            device_id=(peer, cd),
            device_id_type=MESH,
        )

    def item_arrived(half, du, y):
        item_copy(0, half, ab, place(half, du, 0, y)).wait_recv()

    def pair_arrived(half, du, dv):
        pair_copy(0, half, ab, place(half, du, dv, 0)).wait_recv()

    def forward(i, half, du, dv, to):
        pair_copy(i, half, place(half, 0, to, pick), place(half, du, dv, 0)).start()

    pl.semaphore_wait(barrier, 16)

    for n, (du, dy) in enumerate(plane):
        for half in range(2):
            item_copy(2 * n + half, half, peer_of(half, du, dy), ab).start()

    acc[...] = jnp.zeros_like(acc)

    for half in range(2):
        item_arrived(half, 0, 1 - pick)
        forward(14 + 2 * half, half, 0, 0, 1)
        forward(15 + 2 * half, half, 0, 0, 3)
    for n, du in enumerate((1, 3, 2)):
        for half in range(2):
            item_arrived(half, du, 0)
            item_arrived(half, du, 1)
            forward(18 + 4 * n + 2 * half, half, du, 0, 1)
            forward(19 + 4 * n + 2 * half, half, du, 0, 3)

    low_half = lax.rem(iota((8, 256), 1), 16) < 8

    def tile(dx, dz):
        source = lax.rem(irrep + dx, 4)
        second = source ^ irrep ^ cd
        at = lax.rem(ring + dz, 4)
        first = source * GROUP + at * 2
        weights = jnp.concatenate(
            [panels[half, pl.ds(first, 2)].reshape(256, 128) for half in range(2)], axis=1
        )
        first_c = pl.multiple_of(at * 2 * CB, 2 * CB)
        rows = ints[:, pl.ds(second * WIR, WIR), pl.ds(first_c, 2 * CB), :]
        left = jnp.concatenate([rows[:, :, :CB], rows[:, :, CB:]], axis=3)
        left = left.reshape(OWN * WIR * CB, 256)
        term = jnp.dot(left, weights, preferred_element_type=F32)
        term = term.reshape(OWN * WIR, 2, 8, 256)
        acc[second] += jnp.where(low_half[None], term[:, 0], term[:, 1])

    def tiles(count, dx_of, dz_of):
        def body(i, carry):
            tile(dx_of(i), dz_of(i))
            return carry

        lax.fori_loop(0, count, body, 0)

    relays = [(0, 3, 1), (1, 1, 3), (3, 1, 3), (2, 3, 1)]

    def relay(n):
        du, dv, to = relays[n]
        for half in range(2):
            pair_arrived(half, du, dv)
            forward(30 + 2 * n + half, half, du, dv, to)

    relay(0)
    fetch.wait()
    tile(0, 0)
    relay(1)
    relay(2)
    for half in range(2):
        pair_arrived(half, 0, 1)
    tiles(4, lambda i: lax.rem(i // 2 * (2 * i + 1), 4), lambda i: (1 - i // 2) * (2 * i + 1))
    relay(3)
    for half in range(2):
        for du in (1, 3):
            pair_arrived(half, du, 3)
        pair_arrived(half, 2, 1)
    tiles(4, lambda i: i // 2 * 2 + 1, lambda i: lax.rem(i, 2) * 2 + 1)

    diagonal = lax.rem(iota((8, 256), 1), 8) == iota((8, 256), 0)
    spread_pairs = (
        lax.rem(iota((768, 128), 1), 16) == lax.rem(iota((768, 128), 0), 256) // CB
    ).astype(BF16)
    row = iota((72, 128), 0)
    lane = iota((72, 128), 1)
    lane_slot, lane_item = lane // 64, lax.rem(lane, 64) // 16
    row_a, row_b = row // WIR, lax.rem(row, WIR)
    own_keep = (lane_slot == lax.rem(row_b // OWN, 2)) & (lane_item == lax.rem(row_b, OWN))
    msg_keep = (lane_slot == slot_lane) & (lane_item == row_a)
    to = iota((80, 144), 0)
    frm = iota((80, 144), 1)
    frm_row = lax.rem(frm, 72)
    frm_a, frm_b = frm_row // WIR, lax.rem(frm_row, WIR)
    frm_slot, frm_k = frm_b // OWN, lax.rem(frm_b, OWN)
    goal = jnp.where(
        frm < 72,
        (frm_slot // 4) * 8 + lax.rem(frm_slot // 2, 2) * 4 + frm_a,
        16 + frm_slot * 8 + slot_low * 4 + frm_k,
    )
    gather_rows = (to == goal).astype(BF16)
    gather_rows = jnp.concatenate([gather_rows] * 3, axis=1)

    def msg_copy(peer, block, sender):
        return pltpu.make_async_remote_copy(
            src_ref=msgs.at[block],
            dst_ref=mirror.at[sender],
            send_sem=msg_send.at[block],
            recv_sem=msg_recv.at[sender],
            device_id=(peer, cd),
            device_id_type=MESH,
        )

    def finish(dx):
        second = lax.rem(irrep + dx, 4) ^ irrep ^ cd
        folded = jnp.sum(jnp.where(diagonal[None], acc[second], 0.0), axis=1)
        values = jnp.dot(split3(folded, 1), spread_pairs, preferred_element_type=F32)
        both = jnp.concatenate(
            [jnp.where(own_keep, values, 0.0), jnp.where(msg_keep, values, 0.0)], axis=0
        )
        placed = jnp.dot(gather_rows, split3(both, 0), preferred_element_type=F32)
        own[second] = placed[:16].reshape(2, 8, 128)
        msgs[pl.ds(second * GROUP, GROUP)] = placed[16:].reshape(GROUP, 8, 128)

        def send(i, inner):
            peer = second * GROUP + i

            @pl.when(peer != ab)
            def _():
                msg_copy(peer, peer, ab).start()

            return inner

        lax.fori_loop(0, GROUP, send, 0)

    for half in range(2):
        pair_arrived(half, 0, 2)
    tile(0, 2)
    finish(0)
    for half in range(2):
        for du in (1, 3):
            pair_arrived(half, du, 2)
        pair_arrived(half, 2, 2)

    def rest(i, carry):
        dx = 2 * i + 1
        tile(dx, 2)
        finish(dx)
        return carry

    lax.fori_loop(0, 2, rest, 0)
    tiles(4, lambda i: 2, lambda i: i)
    finish(2)
    mirror[ab] = msgs[ab]

    def collect(i, carry):
        msg_copy(ab, ab, ab ^ i).wait_recv()
        return carry

    lax.fori_loop(1, 32, collect, 0)
    total = own[...] + jnp.sum(mirror[...].reshape(IRREPS, 2, 4, 8, 128), axis=2)
    shares[cd] = total

    def share_copy(i, peer, sender):
        return pltpu.make_async_remote_copy(
            src_ref=shares.at[sender],
            dst_ref=shares.at[sender],
            send_sem=share_send.at[i],
            recv_sem=share_recv.at[sender],
            device_id=(ab, peer),
            device_id_type=MESH,
        )

    for i in range(1, 4):
        share_copy(i, cd ^ i, cd).start()
    for i in range(1, 4):
        share_copy(i, cd, cd ^ i).wait_recv()
    out[...] = (shares[0] + shares[1]) + (shares[2] + shares[3])

    def sent_items(i, carry):
        item_copy(i, 0, ab, ab).wait_send()
        return carry

    def sent_pairs(i, carry):
        pair_copy(i, 0, ab, 0).wait_send()
        return carry

    def sent_msgs(i, carry):
        msg_copy(ab, ab ^ i, ab).wait_send()
        return carry

    lax.fori_loop(0, 14, sent_items, 0)
    lax.fori_loop(14, 38, sent_pairs, 0)
    lax.fori_loop(1, 32, sent_msgs, 0)
    for i in range(1, 4):
        share_copy(i, cd, cd).wait_send()


def on_device(integrals, amplitudes, block_sizes):
    vmem = pl.BlockSpec(memory_space=pltpu.VMEM)
    packed = pl.pallas_call(
        kernel,
        out_shape=jax.ShapeDtypeStruct((IRREPS, 2, 8, 128), F32),
        in_specs=[
            pl.BlockSpec(memory_space=pltpu.SMEM),
            pl.BlockSpec(memory_space=pl.ANY),
            pl.BlockSpec(memory_space=pl.ANY),
        ],
        out_specs=vmem,
        scratch_shapes=[
            pltpu.VMEM(integrals.shape, BF16),
            pltpu.VMEM(amplitudes.shape, BF16),
            pltpu.VMEM((2, 32, BLK, NPAIR * CB // 2), BF16),
            pltpu.VMEM((IRREPS, OWN * WIR, 8, 256), F32),
            pltpu.VMEM((IRREPS, 2, 8, 128), F32),
            pltpu.VMEM((32, 8, 128), F32),
            pltpu.VMEM((32, 8, 128), F32),
            pltpu.VMEM((4, IRREPS, 2, 8, 128), F32),
            pltpu.SemaphoreType.DMA,
            pltpu.SemaphoreType.DMA,
            pltpu.SemaphoreType.DMA((38,)),
            pltpu.SemaphoreType.DMA((2, 32)),
            pltpu.SemaphoreType.DMA((2, 16)),
            pltpu.SemaphoreType.DMA((32,)),
            pltpu.SemaphoreType.DMA((32,)),
            pltpu.SemaphoreType.DMA((4,)),
            pltpu.SemaphoreType.DMA((4,)),
        ],
        compiler_params=pltpu.CompilerParams(
            collective_id=0, has_side_effects=True, vmem_limit_bytes=56 << 20
        ),
        name="ladder",
    )(block_sizes, amplitudes, integrals)
    packed = packed.reshape(IRREPS, 2, 2, 4, 2, 4, NPAIR)[:, :, :, :OWN, :, :OWN]
    return packed.transpose(6, 3, 0, 1, 2, 4, 5).reshape(NPAIR, OWN, IRREPS * WIR)


def solution(mesh):
    placed = (P("ab", None, None, "cd"), P(None, "ab", "cd"), P())
    return jax.shard_map(
        on_device, mesh=mesh, in_specs=placed, out_specs=P(None, "ab", None), check_vma=False
    )
```

```python
import jax
import jax.numpy as jnp
from jax import lax
from jax.experimental import pallas as pl
from jax.experimental.pallas import tpu as pltpu
from jax.sharding import PartitionSpec as P

IRREPS = 4
BLK = 128
NPAIR = 16
WIR = 24
GROUP = 8
OWN = 3
CB = 16
MESH = pl.DeviceIdType.MESH
F32 = jnp.float32
BF16 = jnp.bfloat16


def iota(shape, dim):
    return lax.broadcasted_iota(jnp.int32, shape, dim)


def split2(x, axis):
    high = x.astype(BF16)
    low = (x - high.astype(F32)).astype(BF16)
    return jnp.concatenate([high, low], axis=axis)


def kernel(
    sizes, amps, integrals, out, ints, plain, panels, acc, msgs, mirror, shares, lates,
    ints_sem, plain_sem, send_sem, item_recv, pair_recv, msg_send, msg_recv,
    share_send, share_recv, late_send, late_recv, token,
):
    ab = lax.axis_index("ab")
    cd = lax.axis_index("cd")
    irrep = ab // GROUP
    slot = lax.rem(ab, GROUP)
    slot_low = lax.rem(slot // 2, 2)
    slot_lane = lax.rem(slot, 2)
    ring = slot // 2
    pick = slot_lane
    core = lax.rem(cd, 2)
    late = cd ^ 2

    fetch_own = pltpu.make_async_copy(amps, plain, plain_sem)
    fetch_own.start()

    def place(half, du, dv, y):
        if half == 0:
            return lax.rem(irrep + dv, 4) * GROUP + lax.rem(ring + du, 4) * 2 + y
        return lax.rem(irrep + du, 4) * GROUP + lax.rem(ring + dv, 4) * 2 + y

    plane = [(0, 1), (1, 0), (3, 0), (1, 1), (3, 1), (2, 0), (2, 1)]

    def peer_of(half, du, dy):
        return place(half, du, 0, lax.rem(pick + dy, 2))

    barrier = pltpu.get_barrier_semaphore()
    for half in range(2):
        for du, dy in plane[half:]:
            pl.semaphore_signal(
                barrier, inc=1, device_id=(peer_of(half, du, dy), cd), device_id_type=MESH
            )
    for i in range(1, 4):
        pl.semaphore_signal(barrier, inc=1, device_id=(ab, cd ^ i), device_id_type=MESH)

    fetch = pltpu.make_async_copy(integrals, ints, ints_sem)
    fetch.start()

    row_limit = sizes[irrep] - slot * CB
    col_limit = sizes[cd]
    shape = (NPAIR * CB, BLK)
    keep = (lax.rem(iota(shape, 0), CB) < row_limit) & (iota(shape, 1) < col_limit)
    fetch_own.wait()
    turned = jnp.where(keep, plain[...].reshape(shape).astype(F32), 0.0).T.astype(BF16)
    panels[0, ab] = turned[:, :128]
    panels[1, ab] = turned[:, 128:]

    def item_copy(i, half, peer, block):
        return pltpu.make_async_remote_copy(
            src_ref=panels.at[half, block],
            dst_ref=panels.at[half, block],
            send_sem=send_sem.at[i],
            recv_sem=item_recv.at[half, block],
            device_id=(peer, cd),
            device_id_type=MESH,
        )

    def pair_copy(i, half, peer, first):
        return pltpu.make_async_remote_copy(
            src_ref=panels.at[half, pl.ds(first, 2)],
            dst_ref=panels.at[half, pl.ds(first, 2)],
            send_sem=send_sem.at[i],
            recv_sem=pair_recv.at[half, first // 2],
            device_id=(peer, cd),
            device_id_type=MESH,
        )

    def item_arrived(half, du, y):
        item_copy(0, half, ab, place(half, du, 0, y)).wait_recv()

    def pair_arrived(half, du, dv):
        pair_copy(0, half, ab, place(half, du, dv, 0)).wait_recv()

    def forward(i, half, du, dv, to):
        pair_copy(i, half, place(half, 0, to, pick), place(half, du, dv, 0)).start()

    pl.semaphore_wait(barrier, 16)

    for n, (du, dy) in enumerate(plane):
        for half in range(2):
            item_copy(2 * n + half, half, peer_of(half, du, dy), ab).start()

    acc[...] = jnp.zeros_like(acc)
    shares[cd, late] = jnp.zeros((2, 8, 128), F32)

    for half in range(2):
        item_arrived(half, 0, 1 - pick)
        forward(14 + 2 * half, half, 0, 0, 1)
        forward(15 + 2 * half, half, 0, 0, 3)
    for n, du in enumerate((1, 3, 2)):
        for half in range(2):
            item_arrived(half, du, 0)
            item_arrived(half, du, 1)
            forward(18 + 4 * n + 2 * half, half, du, 0, 1)
            forward(19 + 4 * n + 2 * half, half, du, 0, 3)
    pl.semaphore_signal(token, inc=1, device_id=(ab, cd ^ 1), device_id_type=MESH)

    low_half = lax.rem(iota((8, 256), 1), 16) < 8

    def tile(dx, dz):
        source = lax.rem(irrep + dx, 4)
        second = source ^ irrep ^ cd
        at = lax.rem(ring + dz, 4)
        first = source * GROUP + at * 2
        weights = jnp.concatenate(
            [panels[half, pl.ds(first, 2)].reshape(256, 128) for half in range(2)], axis=1
        )
        first_c = pl.multiple_of(at * 2 * CB, 2 * CB)
        rows = ints[:, pl.ds(second * WIR, WIR), pl.ds(first_c, 2 * CB), :]
        left = jnp.concatenate([rows[:, :, :CB], rows[:, :, CB:]], axis=3)
        left = left.reshape(OWN * WIR * CB, 256)
        term = jnp.dot(left, weights, preferred_element_type=F32)
        term = term.reshape(OWN * WIR, 2, 8, 256)
        acc[second] += jnp.where(low_half[None], term[:, 0], term[:, 1])

    relays = [(0, 3, 1), (1, 1, 3), (3, 1, 3), (2, 3, 1)]

    def relay(n):
        du, dv, to = relays[n]
        for half in range(2):
            pair_arrived(half, du, dv)
            forward(30 + 2 * n + half, half, du, dv, to)

    relay(0)
    fetch.wait()
    tile(0, 0)
    relay(1)
    relay(2)
    for half in range(2):
        pair_arrived(half, 0, 1)
    for dx, dz in ((0, 1), (0, 3), (1, 0), (3, 0)):
        tile(dx, dz)
    relay(3)
    for half in range(2):
        for du in (1, 3):
            pair_arrived(half, du, 3)
        pair_arrived(half, 2, 1)
    for dx, dz in ((1, 1), (1, 3), (3, 1), (3, 3)):
        tile(dx, dz)

    diagonal = lax.rem(iota((8, 256), 1), 8) == iota((8, 256), 0)
    spread_pairs = (
        lax.rem(iota((512, 128), 1), 16) == lax.rem(iota((512, 128), 0), 256) // CB
    ).astype(BF16)
    row = iota((72, 128), 0)
    lane = iota((72, 128), 1)
    lane_slot, lane_item = lane // 64, lax.rem(lane, 64) // 16
    row_a, row_b = row // WIR, lax.rem(row, WIR)
    own_keep = (lane_slot == lax.rem(row_b // OWN, 2)) & (lane_item == lax.rem(row_b, OWN))
    msg_keep = (lane_slot == slot_lane) & (lane_item == row_a)
    to = iota((80, 144), 0)
    frm = iota((80, 144), 1)
    frm_row = lax.rem(frm, 72)
    frm_a, frm_b = frm_row // WIR, lax.rem(frm_row, WIR)
    frm_slot, frm_k = frm_b // OWN, lax.rem(frm_b, OWN)
    goal = jnp.where(
        frm < 72,
        (frm_slot // 4) * 8 + lax.rem(frm_slot // 2, 2) * 4 + frm_a,
        16 + frm_slot * 8 + slot_low * 4 + frm_k,
    )
    gather_rows = (to == goal).astype(BF16)
    gather_rows = jnp.concatenate([gather_rows] * 2, axis=1)

    to_copy = cd // 2 * 2 + lax.rem(irrep, 2)

    def sender_tile(of_irrep, of_core, of_slot):
        return (of_irrep // 2 * 2 + of_core) * GROUP + of_slot

    def msg_copy(peer, block, tile_at):
        return pltpu.make_async_remote_copy(
            src_ref=msgs.at[block],
            dst_ref=mirror.at[tile_at],
            send_sem=msg_send.at[block],
            recv_sem=msg_recv.at[tile_at],
            device_id=(peer, to_copy),
            device_id_type=MESH,
        )

    my_tile = sender_tile(irrep, core, slot)
    stays = to_copy == cd

    def finish(dx):
        second = lax.rem(irrep + dx, 4) ^ irrep ^ cd
        folded = jnp.sum(jnp.where(diagonal[None], acc[second], 0.0), axis=1)
        values = jnp.dot(split2(folded, 1), spread_pairs, preferred_element_type=F32)
        both = jnp.concatenate(
            [jnp.where(own_keep, values, 0.0), jnp.where(msg_keep, values, 0.0)], axis=0
        )
        placed = jnp.dot(gather_rows, split2(both, 0), preferred_element_type=F32)
        tiles = placed[:16].reshape(2, 8, 128)
        if dx == 2:
            lates[cd, pl.ds(0, 2)] = tiles
        else:
            shares[cd, second] = tiles
        msgs[pl.ds(second * GROUP, GROUP)] = placed[16:].reshape(GROUP, 8, 128)
        for i in range(GROUP):
            peer = second * GROUP + i

            @pl.when((peer != ab) | ~stays)
            def _():
                msg_copy(peer, peer, my_tile).start()

    def share_copy(i, peer, sender):
        return pltpu.make_async_remote_copy(
            src_ref=shares.at[sender],
            dst_ref=shares.at[sender],
            send_sem=share_send.at[i],
            recv_sem=share_recv.at[sender],
            device_id=(ab, peer),
            device_id_type=MESH,
        )

    def late_copy(i, peer, sender):
        return pltpu.make_async_remote_copy(
            src_ref=lates.at[sender],
            dst_ref=lates.at[sender],
            send_sem=late_send.at[i],
            recv_sem=late_recv.at[sender],
            device_id=(ab, peer),
            device_id_type=MESH,
        )

    pl.semaphore_wait(token, 1)
    for half in range(2):
        pair_arrived(half, 0, 2)
    tile(0, 2)
    finish(0)
    for half in range(2):
        for du in (1, 3):
            pair_arrived(half, du, 2)
    for dx, dz in ((1, 2), (3, 2), (2, 0), (2, 1), (2, 3)):
        tile(dx, dz)
    for dx in (1, 3):
        finish(dx)
    for i in range(1, 4):
        share_copy(i, cd ^ i, cd).start()
    for half in range(2):
        pair_arrived(half, 2, 2)
    tile(2, 2)
    finish(2)

    @pl.when(stays)
    def _():
        mirror[my_tile] = msgs[ab]

    def collect(i, carry):
        @pl.when((i != my_tile) | ~stays)
        def _():
            msg_copy(ab, ab, i).wait_recv()

        return carry

    lax.fori_loop(0, 32, collect, 0)
    lates[cd, pl.ds(2, 4)] = jnp.sum(
        mirror[...].reshape(2, 2, 2, 4, 8, 128), axis=(1, 3)
    ).reshape(4, 8, 128)
    for i in range(1, 4):
        late_copy(i, cd ^ i, cd).start()
    for i in range(1, 4):
        share_copy(i, cd, cd ^ i).wait_recv()
    early = (shares[0] + shares[1]) + (shares[2] + shares[3])
    for i in range(1, 4):
        late_copy(i, cd, cd ^ i).wait_recv()
    for second in range(IRREPS):
        at = pl.ds(2 + second // 2 * 2, 2)
        odd = second % 2
        out[second] = (
            (early[second] + lates[second ^ 2, pl.ds(0, 2)]) + (lates[odd, at] + lates[odd + 2, at])
        )

    def sent_items(i, carry):
        item_copy(i, 0, ab, ab).wait_send()
        return carry

    def sent_pairs(i, carry):
        pair_copy(i, 0, ab, 0).wait_send()
        return carry

    def sent_msgs(i, carry):
        @pl.when((i != ab) | ~stays)
        def _():
            msg_copy(ab, i, my_tile).wait_send()

        return carry

    lax.fori_loop(0, 14, sent_items, 0)
    lax.fori_loop(14, 38, sent_pairs, 0)
    lax.fori_loop(0, 32, sent_msgs, 0)
    for i in range(1, 4):
        share_copy(i, cd, cd).wait_send()
        late_copy(i, cd, cd).wait_send()


def on_device(integrals, amplitudes, block_sizes):
    vmem = pl.BlockSpec(memory_space=pltpu.VMEM)
    packed = pl.pallas_call(
        kernel,
        out_shape=jax.ShapeDtypeStruct((IRREPS, 2, 8, 128), F32),
        in_specs=[
            pl.BlockSpec(memory_space=pltpu.SMEM),
            pl.BlockSpec(memory_space=pl.ANY),
            pl.BlockSpec(memory_space=pl.ANY),
        ],
        out_specs=vmem,
        scratch_shapes=[
            pltpu.VMEM(integrals.shape, BF16),
            pltpu.VMEM(amplitudes.shape, BF16),
            pltpu.VMEM((2, 32, BLK, NPAIR * CB // 2), BF16),
            pltpu.VMEM((IRREPS, OWN * WIR, 8, 256), F32),
            pltpu.VMEM((32, 8, 128), F32),
            pltpu.VMEM((32, 8, 128), F32),
            pltpu.VMEM((4, IRREPS, 2, 8, 128), F32),
            pltpu.VMEM((4, 6, 8, 128), F32),
            pltpu.SemaphoreType.DMA,
            pltpu.SemaphoreType.DMA,
            pltpu.SemaphoreType.DMA((38,)),
            pltpu.SemaphoreType.DMA((2, 32)),
            pltpu.SemaphoreType.DMA((2, 16)),
            pltpu.SemaphoreType.DMA((32,)),
            pltpu.SemaphoreType.DMA((32,)),
            pltpu.SemaphoreType.DMA((4,)),
            pltpu.SemaphoreType.DMA((4,)),
            pltpu.SemaphoreType.DMA((4,)),
            pltpu.SemaphoreType.DMA((4,)),
            pltpu.SemaphoreType.REGULAR,
        ],
        compiler_params=pltpu.CompilerParams(
            collective_id=0, has_side_effects=True, vmem_limit_bytes=56 << 20
        ),
        name="ladder",
    )(block_sizes, amplitudes, integrals)
    packed = packed.reshape(IRREPS, 2, 2, 4, 2, 4, NPAIR)[:, :, :, :OWN, :, :OWN]
    return packed.transpose(6, 3, 0, 1, 2, 4, 5).reshape(NPAIR, OWN, IRREPS * WIR)


def solution(mesh):
    placed = (P("ab", None, None, "cd"), P(None, "ab", "cd"), P())
    return jax.shard_map(
        on_device, mesh=mesh, in_specs=placed, out_specs=P(None, "ab", None), check_vma=False
    )
```

```python
import jax
import jax.numpy as jnp
from jax import lax
from jax.experimental import pallas as pl
from jax.experimental.pallas import tpu as pltpu
from jax.sharding import PartitionSpec as P

IRREPS = 4
BLK = 128
NPAIR = 16
WIR = 24
GROUP = 8
OWN = 3
CB = 16
MESH = pl.DeviceIdType.MESH
F32 = jnp.float32
BF16 = jnp.bfloat16


def iota(shape, dim):
    return lax.broadcasted_iota(jnp.int32, shape, dim)


def split2(x, axis):
    high = x.astype(BF16)
    low = (x - high.astype(F32)).astype(BF16)
    return jnp.concatenate([high, low], axis=axis)


def kernel(
    sizes, amps, integrals, out, ints, plain, panels, acc, given, taken, msgs, mirror, own, halves,
    ints_sem, plain_sem, send_sem, item_recv, pair_recv, pass_send, pass_recv,
    msg_send, msg_recv, own_send, own_recv, half_send, half_recv, token,
):
    ab = lax.axis_index("ab")
    cd = lax.axis_index("cd")
    irrep = ab // GROUP
    slot = lax.rem(ab, GROUP)
    slot_low = lax.rem(slot // 2, 2)
    slot_lane = lax.rem(slot, 2)
    ring = slot // 2
    pick = slot_lane
    core = lax.rem(cd, 2)
    high = cd // 2
    other = cd ^ 1

    fetch_own = pltpu.make_async_copy(amps, plain, plain_sem)
    fetch_own.start()

    def place(half, du, dv, y):
        if half == 0:
            return lax.rem(irrep + dv, 4) * GROUP + lax.rem(ring + du, 4) * 2 + y
        return lax.rem(irrep + du, 4) * GROUP + lax.rem(ring + dv, 4) * 2 + y

    plane = [(0, 1), (1, 0), (3, 0), (1, 1), (3, 1), (2, 0), (2, 1)]

    def peer_of(half, du, dy):
        return place(half, du, 0, lax.rem(pick + dy, 2))

    barrier = pltpu.get_barrier_semaphore()
    for half in range(2):
        for du, dy in plane[half:]:
            pl.semaphore_signal(
                barrier, inc=1, device_id=(peer_of(half, du, dy), cd), device_id_type=MESH
            )
    for i in range(1, 4):
        pl.semaphore_signal(barrier, inc=1, device_id=(ab, cd ^ i), device_id_type=MESH)

    fetch = pltpu.make_async_copy(integrals, ints, ints_sem)
    fetch.start()

    row_limit = sizes[irrep] - slot * CB
    col_limit = sizes[cd]
    shape = (NPAIR * CB, BLK)
    keep = (lax.rem(iota(shape, 0), CB) < row_limit) & (iota(shape, 1) < col_limit)
    fetch_own.wait()
    turned = jnp.where(keep, plain[...].reshape(shape).astype(F32), 0.0).T.astype(BF16)
    panels[0, ab] = turned[:, :128]
    panels[1, ab] = turned[:, 128:]

    def item_copy(i, half, peer, block):
        return pltpu.make_async_remote_copy(
            src_ref=panels.at[half, block],
            dst_ref=panels.at[half, block],
            send_sem=send_sem.at[i],
            recv_sem=item_recv.at[half, block],
            device_id=(peer, cd),
            device_id_type=MESH,
        )

    def pair_copy(i, half, peer, first):
        return pltpu.make_async_remote_copy(
            src_ref=panels.at[half, pl.ds(first, 2)],
            dst_ref=panels.at[half, pl.ds(first, 2)],
            send_sem=send_sem.at[i],
            recv_sem=pair_recv.at[half, first // 2],
            device_id=(peer, cd),
            device_id_type=MESH,
        )

    def item_arrived(half, du, y):
        item_copy(0, half, ab, place(half, du, 0, y)).wait_recv()

    def pair_arrived(half, du, dv):
        pair_copy(0, half, ab, place(half, du, dv, 0)).wait_recv()

    def forward(i, half, du, dv, to):
        pair_copy(i, half, place(half, 0, to, pick), place(half, du, dv, 0)).start()

    pl.semaphore_wait(barrier, 16)

    for n, (du, dy) in enumerate(plane):
        for half in range(2):
            item_copy(2 * n + half, half, peer_of(half, du, dy), ab).start()

    acc[...] = jnp.zeros_like(acc)

    for half in range(2):
        item_arrived(half, 0, 1 - pick)
        forward(14 + 2 * half, half, 0, 0, 1)
        forward(15 + 2 * half, half, 0, 0, 3)
    for n, du in enumerate((1, 3, 2)):
        for half in range(2):
            item_arrived(half, du, 0)
            item_arrived(half, du, 1)
            forward(18 + 4 * n + 2 * half, half, du, 0, 1)
            forward(19 + 4 * n + 2 * half, half, du, 0, 3)
    for i in range(1, 4):
        pl.semaphore_signal(token, inc=1, device_id=(ab, cd ^ i), device_id_type=MESH)

    low_half = lax.rem(iota((8, 256), 1), 16) < 8

    def tile(rel, dz):
        source = irrep ^ rel
        second = source ^ irrep ^ cd
        at = lax.rem(ring + dz, 4)
        first = source * GROUP + at * 2
        weights = jnp.concatenate(
            [panels[half, pl.ds(first, 2)].reshape(256, 128) for half in range(2)], axis=1
        )
        first_c = pl.multiple_of(at * 2 * CB, 2 * CB)
        rows = ints[:, pl.ds(second * WIR, WIR), pl.ds(first_c, 2 * CB), :]
        left = jnp.concatenate([rows[:, :, :CB], rows[:, :, CB:]], axis=3)
        left = left.reshape(OWN * WIR * CB, 256)
        term = jnp.dot(left, weights, preferred_element_type=F32)
        term = term.reshape(OWN * WIR, 2, 8, 256)
        acc[second] += jnp.where(low_half[None], term[:, 0], term[:, 1])

    relays = [(0, 3, 1), (1, 1, 3), (3, 1, 3), (2, 3, 1)]

    def relay(n):
        du, dv, to = relays[n]
        for half in range(2):
            pair_arrived(half, du, dv)
            forward(30 + 2 * n + half, half, du, dv, to)

    relay(0)
    fetch.wait()
    tile(0, 0)
    relay(1)
    relay(2)
    for half in range(2):
        pair_arrived(half, 0, 1)
    for rel, dz in ((0, 1), (0, 3), (1, 0), (3, 0)):
        tile(rel, dz)
    relay(3)
    for half in range(2):
        for du in (1, 3):
            pair_arrived(half, du, 3)
        pair_arrived(half, 2, 1)
    for rel, dz in ((1, 1), (1, 3), (3, 1), (3, 3)):
        tile(rel, dz)

    diagonal = lax.rem(iota((8, 256), 1), 8) == iota((8, 256), 0)
    spread_pairs = (
        lax.rem(iota((512, 128), 1), 16) == lax.rem(iota((512, 128), 0), 256) // CB
    ).astype(BF16)
    row = iota((72, 128), 0)
    lane = iota((72, 128), 1)
    lane_slot, lane_item = lane // 64, lax.rem(lane, 64) // 16
    row_a, row_b = row // WIR, lax.rem(row, WIR)
    own_keep = (lane_slot == lax.rem(row_b // OWN, 2)) & (lane_item == lax.rem(row_b, OWN))
    msg_keep = (lane_slot == slot_lane) & (lane_item == row_a)
    to = iota((80, 144), 0)
    frm = iota((80, 144), 1)
    frm_row = lax.rem(frm, 72)
    frm_a, frm_b = frm_row // WIR, lax.rem(frm_row, WIR)
    frm_slot, frm_k = frm_b // OWN, lax.rem(frm_b, OWN)
    goal = jnp.where(
        frm < 72,
        (frm_slot // 4) * 8 + lax.rem(frm_slot // 2, 2) * 4 + frm_a,
        16 + frm_slot * 8 + slot_low * 4 + frm_k,
    )
    gather_rows = (to == goal).astype(BF16)
    gather_rows = jnp.concatenate([gather_rows] * 2, axis=1)

    to_core = lax.rem(irrep, 2)

    def pass_copy(n, peer):
        return pltpu.make_async_remote_copy(
            src_ref=given.at[n],
            dst_ref=taken.at[n],
            send_sem=pass_send.at[n],
            recv_sem=pass_recv.at[n],
            device_id=(ab, peer),
            device_id_type=MESH,
        )

    def msg_copy(block, to_high, tile_at):
        return pltpu.make_async_remote_copy(
            src_ref=msgs.at[block],
            dst_ref=mirror.at[tile_at],
            send_sem=msg_send.at[to_high, block],
            recv_sem=msg_recv.at[tile_at],
            device_id=(block, to_high * 2 + to_core),
            device_id_type=MESH,
        )

    my_tile = (irrep // 2 * 2 + high) * GROUP + slot
    stays = to_core == core

    def own_copy(n, peer, sender):
        return pltpu.make_async_remote_copy(
            src_ref=own.at[sender, n],
            dst_ref=own.at[sender, n],
            send_sem=own_send.at[n],
            recv_sem=own_recv.at[n],
            device_id=(ab, peer),
            device_id_type=MESH,
        )

    def half_copy(peer, sender):
        return pltpu.make_async_remote_copy(
            src_ref=halves.at[sender],
            dst_ref=halves.at[sender],
            send_sem=half_send,
            recv_sem=half_recv,
            device_id=(ab, peer),
            device_id_type=MESH,
        )

    def finish(rel):
        second = rel ^ cd
        folded = jnp.sum(jnp.where(diagonal[None], acc[second], 0.0), axis=1)
        values = jnp.dot(split2(folded, 1), spread_pairs, preferred_element_type=F32)
        both = jnp.concatenate(
            [jnp.where(own_keep, values, 0.0), jnp.where(msg_keep, values, 0.0)], axis=0
        )
        placed = jnp.dot(gather_rows, split2(both, 0), preferred_element_type=F32)
        if rel % 2:
            given[rel // 2] = placed
            pass_copy(rel // 2, other).start()
            return
        pass_copy(rel // 2, other).wait_recv()
        placed = placed + taken[rel // 2]
        msgs[pl.ds(second * GROUP, GROUP)] = placed[16:].reshape(GROUP, 8, 128)
        for i in range(GROUP):
            block = second * GROUP + i
            for to_high in range(2):

                @pl.when((block != ab) | (to_high * 2 + to_core != cd))
                def _():
                    msg_copy(block, to_high, my_tile).start()

        at = second // 2
        own[high, at] = placed[:16].reshape(2, 8, 128)
        own_copy(at, cd ^ 2, high).start()

    for half in range(2):
        for du in (0, 1, 3):
            pair_arrived(half, du, 2)
    for rel, dz in ((1, 2), (3, 2), (0, 2), (2, 0), (2, 1), (2, 3)):
        tile(rel, dz)
    finish(1)
    finish(3)
    pl.semaphore_wait(token, 3)
    finish(0)
    for half in range(2):
        pair_arrived(half, 2, 2)
    tile(2, 2)
    finish(2)

    @pl.when(stays)
    def _():
        mirror[my_tile] = msgs[ab]

    def collect(i, carry):
        @pl.when((i != my_tile) | ~stays)
        def _():
            msg_copy(ab, 0, i).wait_recv()

        return carry

    lax.fori_loop(0, 32, collect, 0)
    mirrored = jnp.sum(mirror[...].reshape(2, 2, 2, 4, 8, 128), axis=(1, 3))
    for n in range(2):
        own_copy(n, cd, 1 - high).wait_recv()
    halves[core] = (own[0] + own[1]) + mirrored
    half_copy(other, core).start()
    half_copy(cd, 1 - core).wait_recv()
    for second in range(IRREPS):
        out[second] = halves[second % 2, second // 2]

    def sent_items(i, carry):
        item_copy(i, 0, ab, ab).wait_send()
        return carry

    def sent_pairs(i, carry):
        pair_copy(i, 0, ab, 0).wait_send()
        return carry

    def sent_msgs(i, carry):
        for to_high in range(2):
            for n in range(2):
                block = (core + 2 * n) * GROUP + i

                @pl.when((block != ab) | (to_high * 2 + to_core != cd))
                def _():
                    msg_copy(block, to_high, my_tile).wait_send()

        return carry

    lax.fori_loop(0, 14, sent_items, 0)
    lax.fori_loop(14, 38, sent_pairs, 0)
    lax.fori_loop(0, GROUP, sent_msgs, 0)
    for n in range(2):
        pass_copy(n, cd).wait_send()
        own_copy(n, cd, high).wait_send()
    half_copy(cd, core).wait_send()


def on_device(integrals, amplitudes, block_sizes):
    vmem = pl.BlockSpec(memory_space=pltpu.VMEM)
    packed = pl.pallas_call(
        kernel,
        out_shape=jax.ShapeDtypeStruct((IRREPS, 2, 8, 128), F32),
        in_specs=[
            pl.BlockSpec(memory_space=pltpu.SMEM),
            pl.BlockSpec(memory_space=pl.ANY),
            pl.BlockSpec(memory_space=pl.ANY),
        ],
        out_specs=vmem,
        scratch_shapes=[
            pltpu.VMEM(integrals.shape, BF16),
            pltpu.VMEM(amplitudes.shape, BF16),
            pltpu.VMEM((2, 32, BLK, NPAIR * CB // 2), BF16),
            pltpu.VMEM((IRREPS, OWN * WIR, 8, 256), F32),
            pltpu.VMEM((2, 80, 128), F32),
            pltpu.VMEM((2, 80, 128), F32),
            pltpu.VMEM((32, 8, 128), F32),
            pltpu.VMEM((32, 8, 128), F32),
            pltpu.VMEM((2, 2, 2, 8, 128), F32),
            pltpu.VMEM((2, 2, 2, 8, 128), F32),
            pltpu.SemaphoreType.DMA,
            pltpu.SemaphoreType.DMA,
            pltpu.SemaphoreType.DMA((38,)),
            pltpu.SemaphoreType.DMA((2, 32)),
            pltpu.SemaphoreType.DMA((2, 16)),
            pltpu.SemaphoreType.DMA((2,)),
            pltpu.SemaphoreType.DMA((2,)),
            pltpu.SemaphoreType.DMA((2, 32)),
            pltpu.SemaphoreType.DMA((32,)),
            pltpu.SemaphoreType.DMA((2,)),
            pltpu.SemaphoreType.DMA((2,)),
            pltpu.SemaphoreType.DMA,
            pltpu.SemaphoreType.DMA,
            pltpu.SemaphoreType.REGULAR,
        ],
        compiler_params=pltpu.CompilerParams(
            collective_id=0, has_side_effects=True, vmem_limit_bytes=56 << 20
        ),
        name="ladder",
    )(block_sizes, amplitudes, integrals)
    packed = packed.reshape(IRREPS, 2, 2, 4, 2, 4, NPAIR)[:, :, :, :OWN, :, :OWN]
    return packed.transpose(6, 3, 0, 1, 2, 4, 5).reshape(NPAIR, OWN, IRREPS * WIR)


def solution(mesh):
    placed = (P("ab", None, None, "cd"), P(None, "ab", "cd"), P())
    return jax.shard_map(
        on_device, mesh=mesh, in_specs=placed, out_specs=P(None, "ab", None), check_vma=False
    )
```

```python
import jax
import jax.numpy as jnp
from jax import lax
from jax.experimental import pallas as pl
from jax.experimental.pallas import tpu as pltpu
from jax.sharding import PartitionSpec as P

IRREPS = 4
BLK = 128
NPAIR = 16
WIR = 24
GROUP = 8
OWN = 3
CB = 16
MESH = pl.DeviceIdType.MESH
F32 = jnp.float32
BF16 = jnp.bfloat16


def iota(shape, dim):
    return lax.broadcasted_iota(jnp.int32, shape, dim)


def split2(x, axis):
    high = x.astype(BF16)
    low = (x - high.astype(F32)).astype(BF16)
    return jnp.concatenate([high, low], axis=axis)


def kernel(
    sizes, amps, integrals, out, ints, plain, panels, acc, given, taken, msgs, mirror, own, halves,
    ints_sem, plain_sem, send_sem, item_recv, pass_send, pass_recv,
    msg_send, msg_recv, own_send, own_recv, half_send, half_recv, token,
):
    ab = lax.axis_index("ab")
    cd = lax.axis_index("cd")
    irrep = ab // GROUP
    slot = lax.rem(ab, GROUP)
    slot_low = lax.rem(slot // 2, 2)
    slot_lane = lax.rem(slot, 2)
    ring = slot // 2
    pick = slot_lane
    core = lax.rem(cd, 2)
    high = cd // 2
    other = cd ^ 1

    fetch_own = pltpu.make_async_copy(amps, plain, plain_sem)
    fetch_own.start()

    along_x = [lax.rem(irrep + d, 4) * GROUP for d in range(4)]
    along_z = [lax.rem(ring + d, 4) * 2 for d in range(4)]
    along_y = [pick, 1 - pick]

    def place(half, du, dv, dy):
        if half == 0:
            return along_x[dv] + along_z[du] + along_y[dy]
        return along_x[du] + along_z[dv] + along_y[dy]

    barrier = pltpu.get_barrier_semaphore()
    for du, dv, dy in ((1, 0, 0), (3, 0, 0), (2, 0, 0), (0, 1, 0), (0, 3, 0), (0, 2, 0), (0, 0, 1)):
        pl.semaphore_signal(
            barrier, inc=1, device_id=(place(0, du, dv, dy), cd), device_id_type=MESH
        )
    for i in range(1, 4):
        pl.semaphore_signal(barrier, inc=1, device_id=(ab, cd ^ i), device_id_type=MESH)

    fetch = pltpu.make_async_copy(integrals, ints, ints_sem)
    fetch.start()

    row_limit = sizes[irrep] - slot * CB
    col_limit = sizes[cd]
    shape = (NPAIR * CB, BLK)
    keep = (lax.rem(iota(shape, 0), CB) < row_limit) & (iota(shape, 1) < col_limit)
    fetch_own.wait()
    turned = jnp.where(keep, plain[...].reshape(shape).astype(F32), 0.0).T.astype(BF16)
    panels[0, ab] = turned[:, :128]
    panels[1, ab] = turned[:, 128:]

    def item_copy(i, half, peer, block):
        return pltpu.make_async_remote_copy(
            src_ref=panels.at[half, block],
            dst_ref=panels.at[half, block],
            send_sem=send_sem.at[i],
            recv_sem=item_recv.at[half, block],
            device_id=(peer, cd),
            device_id_type=MESH,
        )

    sent = []

    def send(half, block, to):
        item_copy(len(sent), half, place(half, *to), place(half, *block)).start()
        sent.append(half)

    def arrived(half, *block):
        item_copy(0, half, ab, place(half, *block)).wait_recv()

    def onward(half, du, dy):
        send(half, (du, 0, dy), (0, 1, 0))
        send(half, (du, 0, dy), (0, 3, 0))
        if (du, dy) == (2, 1):
            send(half, (du, 0, dy), (0, 2, 0))

    def first_ring(du):
        for half in range(2):
            arrived(half, du, 0, 0)
            send(half, (du, 0, 0), (0, 0, 1))
            onward(half, du, 0)

    def from_partner(du):
        for half in range(2):
            arrived(half, du, 0, 1)
            onward(half, du, 1)

    from_below = ((0, 0), (2, 0), (1, 1), (3, 1))

    def relay(du, dy):
        dv = 3 if (du, dy) in from_below else 1
        for half in range(2):
            arrived(half, du, dv, dy)
            send(half, (du, dv, dy), (0, 4 - dv, 0))

    def rest_arrived(du, dy):
        dv = 1 if (du, dy) in from_below else 3
        for half in range(2):
            arrived(half, du, dv, dy)

    def far_arrived(du):
        for half in range(2):
            for dy in range(2):
                arrived(half, du, 2, dy)

    pl.semaphore_wait(barrier, 10)

    for du in (1, 3):
        for half in range(2):
            send(half, (0, 0, 0), (du, 0, 0))
    for half in range(2):
        onward(half, 0, 0)
    for half in range(2):
        send(half, (0, 0, 0), (0, 0, 1))
    for half in range(2):
        send(half, (0, 0, 0), (2, 0, 0))

    acc[...] = jnp.zeros_like(acc)

    first_ring(1)
    first_ring(3)
    from_partner(0)
    relay(0, 0)
    first_ring(2)
    from_partner(1)
    from_partner(3)

    low_half = lax.rem(iota((8, 256), 1), 16) < 8

    def tile(rel, dz):
        source = irrep ^ rel
        second = source ^ irrep ^ cd
        at = lax.rem(ring + dz, 4)
        first = source * GROUP + at * 2
        weights = jnp.concatenate(
            [panels[half, pl.ds(first, 2)].reshape(256, 128) for half in range(2)], axis=1
        )
        first_c = pl.multiple_of(at * 2 * CB, 2 * CB)
        rows = ints[:, pl.ds(second * WIR, WIR), pl.ds(first_c, 2 * CB), :]
        left = jnp.concatenate([rows[:, :, :CB], rows[:, :, CB:]], axis=3)
        left = left.reshape(OWN * WIR * CB, 256)
        term = jnp.dot(left, weights, preferred_element_type=F32)
        term = term.reshape(OWN * WIR, 2, 8, 256)
        acc[second] += jnp.where(low_half[None], term[:, 0], term[:, 1])

    fetch.wait()
    tile(0, 0)
    relay(1, 0)
    relay(3, 0)
    relay(0, 1)
    from_partner(2)
    for i in range(1, 4):
        pl.semaphore_signal(token, inc=1, device_id=(ab, cd ^ i), device_id_type=MESH)
    rest_arrived(0, 0)
    rest_arrived(0, 1)
    for rel, dz in ((0, 1), (0, 3), (1, 0), (3, 0)):
        tile(rel, dz)
    relay(2, 0)
    relay(1, 1)
    relay(3, 1)
    for du in (1, 3):
        for dy in range(2):
            rest_arrived(du, dy)
    for rel, dz in ((1, 1), (1, 3), (3, 1), (3, 3)):
        tile(rel, dz)
    rest_arrived(2, 0)
    for half in range(2):
        for dv in (1, 3):
            arrived(half, 2, dv, 1)

    diagonal = lax.rem(iota((8, 256), 1), 8) == iota((8, 256), 0)
    spread_pairs = (
        lax.rem(iota((512, 128), 1), 16) == lax.rem(iota((512, 128), 0), 256) // CB
    ).astype(BF16)
    row = iota((72, 128), 0)
    lane = iota((72, 128), 1)
    lane_slot, lane_item = lane // 64, lax.rem(lane, 64) // 16
    row_a, row_b = row // WIR, lax.rem(row, WIR)
    own_keep = (lane_slot == lax.rem(row_b // OWN, 2)) & (lane_item == lax.rem(row_b, OWN))
    msg_keep = (lane_slot == slot_lane) & (lane_item == row_a)
    to = iota((80, 144), 0)
    frm = iota((80, 144), 1)
    frm_row = lax.rem(frm, 72)
    frm_a, frm_b = frm_row // WIR, lax.rem(frm_row, WIR)
    frm_slot, frm_k = frm_b // OWN, lax.rem(frm_b, OWN)
    goal = jnp.where(
        frm < 72,
        (frm_slot // 4) * 8 + lax.rem(frm_slot // 2, 2) * 4 + frm_a,
        16 + frm_slot * 8 + slot_low * 4 + frm_k,
    )
    gather_rows = (to == goal).astype(BF16)
    gather_rows = jnp.concatenate([gather_rows] * 2, axis=1)

    to_core = lax.rem(irrep, 2)

    def pass_copy(n, peer):
        return pltpu.make_async_remote_copy(
            src_ref=given.at[n],
            dst_ref=taken.at[n],
            send_sem=pass_send.at[n],
            recv_sem=pass_recv.at[n],
            device_id=(ab, peer),
            device_id_type=MESH,
        )

    def msg_copy(block, to_high, tile_at):
        return pltpu.make_async_remote_copy(
            src_ref=msgs.at[block],
            dst_ref=mirror.at[tile_at],
            send_sem=msg_send.at[to_high, block],
            recv_sem=msg_recv.at[tile_at],
            device_id=(block, to_high * 2 + to_core),
            device_id_type=MESH,
        )

    my_tile = (irrep // 2 * 2 + high) * GROUP + slot
    stays = to_core == core

    def own_copy(n, peer, sender):
        return pltpu.make_async_remote_copy(
            src_ref=own.at[sender, n],
            dst_ref=own.at[sender, n],
            send_sem=own_send.at[n],
            recv_sem=own_recv.at[n],
            device_id=(ab, peer),
            device_id_type=MESH,
        )

    def half_copy(peer, sender):
        return pltpu.make_async_remote_copy(
            src_ref=halves.at[sender],
            dst_ref=halves.at[sender],
            send_sem=half_send,
            recv_sem=half_recv,
            device_id=(ab, peer),
            device_id_type=MESH,
        )

    def finish(rel):
        second = rel ^ cd
        folded = jnp.sum(jnp.where(diagonal[None], acc[second], 0.0), axis=1)
        values = jnp.dot(split2(folded, 1), spread_pairs, preferred_element_type=F32)
        both = jnp.concatenate(
            [jnp.where(own_keep, values, 0.0), jnp.where(msg_keep, values, 0.0)], axis=0
        )
        placed = jnp.dot(gather_rows, split2(both, 0), preferred_element_type=F32)
        if rel % 2:
            given[rel // 2] = placed
            pass_copy(rel // 2, other).start()
            return
        pass_copy(rel // 2, other).wait_recv()
        placed = placed + taken[rel // 2]
        msgs[pl.ds(second * GROUP, GROUP)] = placed[16:].reshape(GROUP, 8, 128)
        for i in range(GROUP):
            block = second * GROUP + i
            for to_high in range(2):

                @pl.when((block != ab) | (to_high * 2 + to_core != cd))
                def _():
                    msg_copy(block, to_high, my_tile).start()

        at = second // 2
        own[high, at] = placed[:16].reshape(2, 8, 128)
        own_copy(at, cd ^ 2, high).start()

    for du in (0, 1, 3):
        far_arrived(du)
    for rel, dz in ((1, 2), (3, 2), (0, 2), (2, 0), (2, 1), (2, 3)):
        tile(rel, dz)
    finish(1)
    finish(3)
    pl.semaphore_wait(token, 3)
    finish(0)
    far_arrived(2)
    tile(2, 2)
    finish(2)

    @pl.when(stays)
    def _():
        mirror[my_tile] = msgs[ab]

    def collect(i, carry):
        @pl.when((i != my_tile) | ~stays)
        def _():
            msg_copy(ab, 0, i).wait_recv()

        return carry

    lax.fori_loop(0, 32, collect, 0)
    mirrored = jnp.sum(mirror[...].reshape(2, 2, 2, 4, 8, 128), axis=(1, 3))
    for n in range(2):
        own_copy(n, cd, 1 - high).wait_recv()
    halves[core] = (own[0] + own[1]) + mirrored
    half_copy(other, core).start()
    half_copy(cd, 1 - core).wait_recv()
    for second in range(IRREPS):
        out[second] = halves[second % 2, second // 2]

    def sent_items(i, carry):
        item_copy(i, 0, ab, ab).wait_send()
        return carry

    def sent_msgs(i, carry):
        for to_high in range(2):
            for n in range(2):
                block = (core + 2 * n) * GROUP + i

                @pl.when((block != ab) | (to_high * 2 + to_core != cd))
                def _():
                    msg_copy(block, to_high, my_tile).wait_send()

        return carry

    lax.fori_loop(0, len(sent), sent_items, 0)
    lax.fori_loop(0, GROUP, sent_msgs, 0)
    for n in range(2):
        pass_copy(n, cd).wait_send()
        own_copy(n, cd, high).wait_send()
    half_copy(cd, core).wait_send()


def on_device(integrals, amplitudes, block_sizes):
    vmem = pl.BlockSpec(memory_space=pltpu.VMEM)
    packed = pl.pallas_call(
        kernel,
        out_shape=jax.ShapeDtypeStruct((IRREPS, 2, 8, 128), F32),
        in_specs=[
            pl.BlockSpec(memory_space=pltpu.SMEM),
            pl.BlockSpec(memory_space=pl.ANY),
            pl.BlockSpec(memory_space=pl.ANY),
        ],
        out_specs=vmem,
        scratch_shapes=[
            pltpu.VMEM(integrals.shape, BF16),
            pltpu.VMEM(amplitudes.shape, BF16),
            pltpu.VMEM((2, 32, BLK, NPAIR * CB // 2), BF16),
            pltpu.VMEM((IRREPS, OWN * WIR, 8, 256), F32),
            pltpu.VMEM((2, 80, 128), F32),
            pltpu.VMEM((2, 80, 128), F32),
            pltpu.VMEM((32, 8, 128), F32),
            pltpu.VMEM((32, 8, 128), F32),
            pltpu.VMEM((2, 2, 2, 8, 128), F32),
            pltpu.VMEM((2, 2, 2, 8, 128), F32),
            pltpu.SemaphoreType.DMA,
            pltpu.SemaphoreType.DMA,
            pltpu.SemaphoreType.DMA((62,)),
            pltpu.SemaphoreType.DMA((2, 32)),
            pltpu.SemaphoreType.DMA((2,)),
            pltpu.SemaphoreType.DMA((2,)),
            pltpu.SemaphoreType.DMA((2, 32)),
            pltpu.SemaphoreType.DMA((32,)),
            pltpu.SemaphoreType.DMA((2,)),
            pltpu.SemaphoreType.DMA((2,)),
            pltpu.SemaphoreType.DMA,
            pltpu.SemaphoreType.DMA,
            pltpu.SemaphoreType.REGULAR,
        ],
        compiler_params=pltpu.CompilerParams(
            collective_id=0, has_side_effects=True, vmem_limit_bytes=56 << 20
        ),
        name="ladder",
    )(block_sizes, amplitudes, integrals)
    packed = packed.reshape(IRREPS, 2, 2, 4, 2, 4, NPAIR)[:, :, :, :OWN, :, :OWN]
    return packed.transpose(6, 3, 0, 1, 2, 4, 5).reshape(NPAIR, OWN, IRREPS * WIR)


def solution(mesh):
    placed = (P("ab", None, None, "cd"), P(None, "ab", "cd"), P())
    return jax.shard_map(
        on_device, mesh=mesh, in_specs=placed, out_specs=P(None, "ab", None), check_vma=False
    )
```

```python
import jax
import jax.numpy as jnp
from jax import lax
from jax.experimental import pallas as pl
from jax.experimental.pallas import tpu as pltpu
from jax.sharding import PartitionSpec as P

IRREPS = 4
BLK = 128
NPAIR = 16
WIR = 24
GROUP = 8
OWN = 3
CB = 16
MESH = pl.DeviceIdType.MESH
F32 = jnp.float32
BF16 = jnp.bfloat16


def iota(shape, dim):
    return lax.broadcasted_iota(jnp.int32, shape, dim)


def split2(x, axis):
    high = x.astype(BF16)
    low = (x - high.astype(F32)).astype(BF16)
    return jnp.concatenate([high, low], axis=axis)


def kernel(
    sizes, amps, integrals, out, ints, plain, panels, acc, given, taken, msgs, mirror, own, halves,
    spread_pairs, keep_rows, gather_rows,
    ints_sem, plain_sem, send_sem, item_recv, pass_send, pass_recv,
    msg_send, msg_recv, own_send, own_recv, half_send, half_recv, token,
):
    ab = lax.axis_index("ab")
    cd = lax.axis_index("cd")
    irrep = ab // GROUP
    slot = lax.rem(ab, GROUP)
    slot_low = lax.rem(slot // 2, 2)
    slot_lane = lax.rem(slot, 2)
    ring = slot // 2
    pick = slot_lane
    core = lax.rem(cd, 2)
    high = cd // 2
    other = cd ^ 1

    fetch_own = pltpu.make_async_copy(amps, plain, plain_sem)
    fetch_own.start()

    along_x = [lax.rem(irrep + d, 4) * GROUP for d in range(4)]
    along_z = [lax.rem(ring + d, 4) * 2 for d in range(4)]
    along_y = [pick, 1 - pick]

    def place(half, du, dv, dy):
        if half == 0:
            return along_x[dv] + along_z[du] + along_y[dy]
        return along_x[du] + along_z[dv] + along_y[dy]

    barrier = pltpu.get_barrier_semaphore()
    for du, dv, dy in ((1, 0, 0), (3, 0, 0), (2, 0, 0), (0, 1, 0), (0, 3, 0), (0, 2, 0), (0, 0, 1)):
        pl.semaphore_signal(
            barrier, inc=1, device_id=(place(0, du, dv, dy), cd), device_id_type=MESH
        )
    for i in range(1, 4):
        pl.semaphore_signal(barrier, inc=1, device_id=(ab, cd ^ i), device_id_type=MESH)

    fetch = pltpu.make_async_copy(integrals, ints, ints_sem)
    fetch.start()

    row_limit = sizes[irrep] - slot * CB
    col_limit = sizes[cd]
    shape = (NPAIR * CB, BLK)
    keep = ((iota(shape, 0) & (CB - 1)) < row_limit) & (iota(shape, 1) < col_limit)
    fetch_own.wait()
    turned = jnp.where(keep, plain[...].reshape(shape).astype(F32), 0.0).T.astype(BF16)
    panels[0, ab] = turned[:, :128]
    panels[1, ab] = turned[:, 128:]

    def item_copy(i, half, peer, block):
        return pltpu.make_async_remote_copy(
            src_ref=panels.at[half, block],
            dst_ref=panels.at[half, block],
            send_sem=send_sem.at[i],
            recv_sem=item_recv.at[half, block],
            device_id=(peer, cd),
            device_id_type=MESH,
        )

    sent = []

    def send(half, block, to):
        item_copy(len(sent), half, place(half, *to), place(half, *block)).start()
        sent.append(half)

    def arrived(half, *block):
        item_copy(0, half, ab, place(half, *block)).wait_recv()

    def onward(half, du, dy):
        send(half, (du, 0, dy), (0, 1, 0))
        send(half, (du, 0, dy), (0, 3, 0))
        if (du, dy) == (2, 1):
            send(half, (du, 0, dy), (0, 2, 0))

    both = (0, 1)

    def first_ring(du, halves=both):
        for half in halves:
            arrived(half, du, 0, 0)
            send(half, (du, 0, 0), (0, 0, 1))
            onward(half, du, 0)

    def from_partner(du, halves=both):
        for half in halves:
            arrived(half, du, 0, 1)
            onward(half, du, 1)

    from_below = ((0, 0), (2, 0), (1, 1), (3, 1))

    def relay(du, dy, halves=both):
        dv = 3 if (du, dy) in from_below else 1
        for half in halves:
            arrived(half, du, dv, dy)
            send(half, (du, dv, dy), (0, 4 - dv, 0))

    def rest_arrived(du, dy, halves=both):
        dv = 1 if (du, dy) in from_below else 3
        for half in halves:
            arrived(half, du, dv, dy)

    def far_arrived(half, du):
        for dy in range(2):
            arrived(half, du, 2, dy)

    pl.semaphore_wait(barrier, 10)

    for du in (1, 3):
        for half in range(2):
            send(half, (0, 0, 0), (du, 0, 0))
    for half in range(2):
        onward(half, 0, 0)
    for half in range(2):
        send(half, (0, 0, 0), (0, 0, 1))
    for half in range(2):
        send(half, (0, 0, 0), (2, 0, 0))

    acc[...] = jnp.zeros_like(acc)
    spread_pairs[...] = (
        (iota((512, 128), 1) & 15) == ((iota((512, 128), 0) & 255) >> 4)
    ).astype(BF16)
    lane = iota((72, 128), 1)
    lane_slot, lane_item = lane >> 6, (lane >> 4) & 3
    row_a, row_b = iota((72, 128), 0) // WIR, lax.rem(iota((72, 128), 0), WIR)
    own_row = (lane_slot == ((row_b // OWN) & 1)) & (lane_item == lax.rem(row_b, OWN))
    keep_rows[pl.ds(0, 72)] = own_row.astype(F32)
    keep_rows[pl.ds(72, 72)] = ((lane_slot == slot_lane) & (lane_item == row_a)).astype(F32)
    frm = iota((80, 144), 1)
    frm_row = lax.rem(frm, 72)
    frm_a, frm_b = frm_row // WIR, lax.rem(frm_row, WIR)
    frm_slot, frm_k = frm_b // OWN, lax.rem(frm_b, OWN)
    goal = jnp.where(
        frm < 72,
        (frm_slot >> 2) * 8 + ((frm_slot >> 1) & 1) * 4 + frm_a,
        16 + frm_slot * 8 + slot_low * 4 + frm_k,
    )
    goal = (iota((80, 144), 0) == goal).astype(BF16)
    gather_rows[...] = jnp.concatenate([goal, goal], axis=1)
    diagonal = (iota((8, 256), 1) & 7) == iota((8, 256), 0)
    low_half = (iota((8, 256), 1) & 15) < 8

    first_ring(1)
    first_ring(3)
    from_partner(0)
    relay(0, 0)
    first_ring(2, (0,))
    from_partner(1)
    from_partner(3)
    from_partner(2, (0,))

    def tile(rel, dz):
        source = irrep ^ rel
        second = source ^ irrep ^ cd
        at = lax.rem(ring + dz, 4)
        first = source * GROUP + at * 2
        weights = jnp.concatenate(
            [panels[half, pl.ds(first, 2)].reshape(256, 128) for half in range(2)], axis=1
        )
        first_c = pl.multiple_of(at * 2 * CB, 2 * CB)
        rows = ints[:, pl.ds(second * WIR, WIR), pl.ds(first_c, 2 * CB), :]
        left = jnp.concatenate([rows[:, :, :CB], rows[:, :, CB:]], axis=3)
        left = left.reshape(OWN * WIR * CB, 256)
        term = jnp.dot(left, weights, preferred_element_type=F32)
        term = term.reshape(OWN * WIR, 2, 8, 256)
        acc[second] += jnp.where(low_half[None], term[:, 0], term[:, 1])

    fetch.wait()
    tile(0, 0)
    relay(1, 0)
    relay(3, 0)
    relay(0, 1)
    first_ring(2, (1,))
    from_partner(2, (1,))
    for i in range(1, 4):
        pl.semaphore_signal(token, inc=1, device_id=(ab, cd ^ i), device_id_type=MESH)
    rest_arrived(0, 0)
    rest_arrived(0, 1)
    for rel, dz in ((0, 1), (0, 3), (1, 0), (3, 0)):
        tile(rel, dz)
    relay(2, 0, (0,))
    relay(1, 1)
    relay(3, 1)
    for du in (1, 3):
        for dy in range(2):
            rest_arrived(du, dy)
    for rel, dz in ((1, 1), (1, 3), (3, 1), (3, 3)):
        tile(rel, dz)
    relay(2, 0, (1,))

    to_core = lax.rem(irrep, 2)

    def pass_copy(n, peer):
        return pltpu.make_async_remote_copy(
            src_ref=given.at[n],
            dst_ref=taken.at[n],
            send_sem=pass_send.at[n],
            recv_sem=pass_recv.at[n],
            device_id=(ab, peer),
            device_id_type=MESH,
        )

    def msg_copy(block, to_high, tile_at):
        return pltpu.make_async_remote_copy(
            src_ref=msgs.at[block],
            dst_ref=mirror.at[tile_at],
            send_sem=msg_send.at[to_high, block],
            recv_sem=msg_recv.at[tile_at],
            device_id=(block, to_high * 2 + to_core),
            device_id_type=MESH,
        )

    my_tile = (irrep // 2 * 2 + high) * GROUP + slot
    stays = to_core == core

    def own_copy(n, peer, sender):
        return pltpu.make_async_remote_copy(
            src_ref=own.at[sender, n],
            dst_ref=own.at[sender, n],
            send_sem=own_send.at[n],
            recv_sem=own_recv.at[n],
            device_id=(ab, peer),
            device_id_type=MESH,
        )

    def half_copy(peer, sender):
        return pltpu.make_async_remote_copy(
            src_ref=halves.at[sender],
            dst_ref=halves.at[sender],
            send_sem=half_send,
            recv_sem=half_recv,
            device_id=(ab, peer),
            device_id_type=MESH,
        )

    def ending(*rels):
        folded = [
            jnp.sum(jnp.where(diagonal[None], acc[rel ^ cd], 0.0), axis=1) for rel in rels
        ]
        values = jnp.dot(
            split2(jnp.concatenate(folded, axis=0), 1),
            spread_pairs[...],
            preferred_element_type=F32,
        )
        kept = []
        for n in range(len(rels)):
            part = values[n * 72 : (n + 1) * 72]
            kept.append(jnp.concatenate([part, part], axis=0) * keep_rows[...])
        return jnp.dot(
            gather_rows[...], split2(jnp.concatenate(kept, axis=1), 0), preferred_element_type=F32
        )

    def finish(rel):
        second = rel ^ cd
        placed = ending(rel)
        pass_copy(rel // 2, other).wait_recv()
        placed = placed + taken[rel // 2]
        msgs[pl.ds(second * GROUP, GROUP)] = placed[16:].reshape(GROUP, 8, 128)
        for i in range(GROUP):
            block = second * GROUP + i
            for to_high in range(2):

                @pl.when((block != ab) | (to_high * 2 + to_core != cd))
                def _():
                    msg_copy(block, to_high, my_tile).start()

        at = second // 2
        own[high, at] = placed[:16].reshape(2, 8, 128)
        own_copy(at, cd ^ 2, high).start()

    far_arrived(1, 0)
    rest_arrived(2, 0, (0,))
    for dv in (1, 3):
        arrived(0, 2, dv, 1)
    far_arrived(1, 1)
    far_arrived(1, 3)
    for rel, dz in ((1, 2), (3, 2), (0, 2)):
        tile(rel, dz)
    passed = ending(1, 3)
    for n in range(2):
        given[n] = passed[:, n * 128 : (n + 1) * 128]
        pass_copy(n, other).start()
    pl.semaphore_wait(token, 3)
    finish(0)
    rest_arrived(2, 0, (1,))
    for dv in (1, 3):
        arrived(1, 2, dv, 1)
    for du in (0, 1, 3):
        far_arrived(0, du)
    for dz in (0, 1, 3):
        tile(2, dz)
    far_arrived(0, 2)
    far_arrived(1, 2)
    tile(2, 2)
    finish(2)

    @pl.when(stays)
    def _():
        mirror[my_tile] = msgs[ab]

    def collect(i, carry):
        @pl.when((i != my_tile) | ~stays)
        def _():
            msg_copy(ab, 0, i).wait_recv()

        return carry

    lax.fori_loop(0, 32, collect, 0)
    mirrored = jnp.sum(mirror[...].reshape(2, 2, 2, 4, 8, 128), axis=(1, 3))
    for n in range(2):
        own_copy(n, cd, 1 - high).wait_recv()
    halves[core] = (own[0] + own[1]) + mirrored
    half_copy(other, core).start()
    half_copy(cd, 1 - core).wait_recv()
    for second in range(IRREPS):
        out[second] = halves[second % 2, second // 2]

    def sent_items(i, carry):
        item_copy(i, 0, ab, ab).wait_send()
        return carry

    def sent_msgs(i, carry):
        for to_high in range(2):
            for n in range(2):
                block = (core + 2 * n) * GROUP + i

                @pl.when((block != ab) | (to_high * 2 + to_core != cd))
                def _():
                    msg_copy(block, to_high, my_tile).wait_send()

        return carry

    lax.fori_loop(0, len(sent), sent_items, 0)
    lax.fori_loop(0, GROUP, sent_msgs, 0)
    for n in range(2):
        pass_copy(n, cd).wait_send()
        own_copy(n, cd, high).wait_send()
    half_copy(cd, core).wait_send()


def on_device(integrals, amplitudes, block_sizes):
    vmem = pl.BlockSpec(memory_space=pltpu.VMEM)
    packed = pl.pallas_call(
        kernel,
        out_shape=jax.ShapeDtypeStruct((IRREPS, 2, 8, 128), F32),
        in_specs=[
            pl.BlockSpec(memory_space=pltpu.SMEM),
            pl.BlockSpec(memory_space=pl.ANY),
            pl.BlockSpec(memory_space=pl.ANY),
        ],
        out_specs=vmem,
        scratch_shapes=[
            pltpu.VMEM(integrals.shape, BF16),
            pltpu.VMEM(amplitudes.shape, BF16),
            pltpu.VMEM((2, 32, BLK, NPAIR * CB // 2), BF16),
            pltpu.VMEM((IRREPS, OWN * WIR, 8, 256), F32),
            pltpu.VMEM((2, 80, 128), F32),
            pltpu.VMEM((2, 80, 128), F32),
            pltpu.VMEM((32, 8, 128), F32),
            pltpu.VMEM((32, 8, 128), F32),
            pltpu.VMEM((2, 2, 2, 8, 128), F32),
            pltpu.VMEM((2, 2, 2, 8, 128), F32),
            pltpu.VMEM((512, 128), BF16),
            pltpu.VMEM((144, 128), F32),
            pltpu.VMEM((80, 288), BF16),
            pltpu.SemaphoreType.DMA,
            pltpu.SemaphoreType.DMA,
            pltpu.SemaphoreType.DMA((62,)),
            pltpu.SemaphoreType.DMA((2, 32)),
            pltpu.SemaphoreType.DMA((2,)),
            pltpu.SemaphoreType.DMA((2,)),
            pltpu.SemaphoreType.DMA((2, 32)),
            pltpu.SemaphoreType.DMA((32,)),
            pltpu.SemaphoreType.DMA((2,)),
            pltpu.SemaphoreType.DMA((2,)),
            pltpu.SemaphoreType.DMA,
            pltpu.SemaphoreType.DMA,
            pltpu.SemaphoreType.REGULAR,
        ],
        compiler_params=pltpu.CompilerParams(
            collective_id=0, has_side_effects=True, vmem_limit_bytes=56 << 20
        ),
        name="ladder",
    )(block_sizes, amplitudes, integrals)
    packed = packed.reshape(IRREPS, 2, 2, 4, 2, 4, NPAIR)[:, :, :, :OWN, :, :OWN]
    return packed.transpose(6, 3, 0, 1, 2, 4, 5).reshape(NPAIR, OWN, IRREPS * WIR)


def solution(mesh):
    placed = (P("ab", None, None, "cd"), P(None, "ab", "cd"), P())
    return jax.shard_map(
        on_device, mesh=mesh, in_specs=placed, out_specs=P(None, "ab", None), check_vma=False
    )
```

```python
import jax
import jax.numpy as jnp
from jax import lax
from jax.experimental import pallas as pl
from jax.experimental.pallas import tpu as pltpu
from jax.sharding import PartitionSpec as P

IRREPS = 4
BLK = 128
NPAIR = 16
WIR = 24
GROUP = 8
OWN = 3
CB = 16
MESH = pl.DeviceIdType.MESH
F32 = jnp.float32
BF16 = jnp.bfloat16


def iota(shape, dim):
    return lax.broadcasted_iota(jnp.int32, shape, dim)


def split2(x, axis):
    high = x.astype(BF16)
    low = (x - high.astype(F32)).astype(BF16)
    return jnp.concatenate([high, low], axis=axis)


def kernel(
    sizes, amps, integrals, out, ints, plain, panels, acc, given, taken, msgs, mirror, own, halves,
    spread_pairs, keep_rows, gather_rows,
    ints_sem, plain_sem, send_sem, item_recv, pass_send, pass_recv,
    msg_send, msg_recv, own_send, own_recv, half_send, half_recv, token,
):
    ab = lax.axis_index("ab")
    cd = lax.axis_index("cd")
    irrep = ab // GROUP
    slot = lax.rem(ab, GROUP)
    slot_low = lax.rem(slot // 2, 2)
    slot_lane = lax.rem(slot, 2)
    ring = slot // 2
    pick = slot_lane
    core = lax.rem(cd, 2)
    high = cd // 2
    other = cd ^ 1

    fetch_own = pltpu.make_async_copy(amps, plain, plain_sem)
    fetch_own.start()

    along_x = [lax.rem(irrep + d, 4) * GROUP for d in range(4)]
    along_z = [lax.rem(ring + d, 4) * 2 for d in range(4)]
    along_y = [pick, 1 - pick]

    def place(half, du, dv, dy):
        if half == 0:
            return along_x[dv] + along_z[du] + along_y[dy]
        return along_x[du] + along_z[dv] + along_y[dy]

    barrier = pltpu.get_barrier_semaphore()
    for du, dv, dy in ((1, 0, 0), (3, 0, 0), (2, 0, 0), (0, 1, 0), (0, 3, 0), (0, 2, 0), (0, 0, 1)):
        pl.semaphore_signal(
            barrier, inc=1, device_id=(place(0, du, dv, dy), cd), device_id_type=MESH
        )
    for i in range(1, 4):
        pl.semaphore_signal(barrier, inc=1, device_id=(ab, cd ^ i), device_id_type=MESH)

    fetch = pltpu.make_async_copy(integrals, ints, ints_sem)
    fetch.start()

    row_limit = sizes[irrep] - slot * CB
    col_limit = sizes[cd]
    shape = (NPAIR * CB, BLK)
    keep = ((iota(shape, 0) & (CB - 1)) < row_limit) & (iota(shape, 1) < col_limit)
    fetch_own.wait()
    turned = jnp.where(keep, plain[...].reshape(shape).astype(F32), 0.0).T.astype(BF16)
    panels[0, ab] = turned[:, :128]
    panels[1, ab] = turned[:, 128:]

    def item_copy(i, half, peer, block):
        return pltpu.make_async_remote_copy(
            src_ref=panels.at[half, block],
            dst_ref=panels.at[half, block],
            send_sem=send_sem.at[i],
            recv_sem=item_recv.at[half, block],
            device_id=(peer, cd),
            device_id_type=MESH,
        )

    sent = []

    def send(half, block, to):
        item_copy(len(sent), half, place(half, *to), place(half, *block)).start()
        sent.append(half)

    def arrived(half, *block):
        item_copy(0, half, ab, place(half, *block)).wait_recv()

    def onward(half, du, dy):
        send(half, (du, 0, dy), (0, 1, 0))
        send(half, (du, 0, dy), (0, 3, 0))
        if (du, dy) == (2, 1):
            send(half, (du, 0, dy), (0, 2, 0))

    both = (0, 1)

    def first_ring(du, halves=both):
        for half in halves:
            arrived(half, du, 0, 0)
            send(half, (du, 0, 0), (0, 0, 1))
            onward(half, du, 0)

    def from_partner(du, halves=both):
        for half in halves:
            arrived(half, du, 0, 1)
            onward(half, du, 1)

    from_below = ((0, 0), (2, 0), (1, 1), (3, 1))

    def relay(du, dy, halves=both):
        dv = 3 if (du, dy) in from_below else 1
        for half in halves:
            arrived(half, du, dv, dy)
            send(half, (du, dv, dy), (0, 4 - dv, 0))

    def rest_arrived(du, dy, halves=both):
        dv = 1 if (du, dy) in from_below else 3
        for half in halves:
            arrived(half, du, dv, dy)

    def far_arrived(half, du):
        for dy in range(2):
            arrived(half, du, 2, dy)

    pl.semaphore_wait(barrier, 10)

    for du in (1, 3):
        for half in range(2):
            send(half, (0, 0, 0), (du, 0, 0))
    for half in range(2):
        onward(half, 0, 0)
    for half in range(2):
        send(half, (0, 0, 0), (0, 0, 1))
    for half in range(2):
        send(half, (0, 0, 0), (2, 0, 0))

    acc[...] = jnp.zeros_like(acc)
    spread_pairs[...] = (
        (iota((512, 128), 1) & 15) == ((iota((512, 128), 0) & 255) >> 4)
    ).astype(BF16)
    lane = iota((72, 128), 1)
    lane_slot, lane_item = lane >> 6, (lane >> 4) & 3
    row_a, row_b = iota((72, 128), 0) // WIR, lax.rem(iota((72, 128), 0), WIR)
    own_row = (lane_slot == ((row_b // OWN) & 1)) & (lane_item == lax.rem(row_b, OWN))
    keep_rows[pl.ds(0, 72)] = own_row.astype(F32)
    keep_rows[pl.ds(72, 72)] = ((lane_slot == slot_lane) & (lane_item == row_a)).astype(F32)
    frm = iota((80, 144), 1)
    frm_row = lax.rem(frm, 72)
    frm_a, frm_b = frm_row // WIR, lax.rem(frm_row, WIR)
    frm_slot, frm_k = frm_b // OWN, lax.rem(frm_b, OWN)
    goal = jnp.where(
        frm < 72,
        (frm_slot >> 2) * 8 + ((frm_slot >> 1) & 1) * 4 + frm_a,
        16 + frm_slot * 8 + slot_low * 4 + frm_k,
    )
    goal = (iota((80, 144), 0) == goal).astype(BF16)
    gather_rows[...] = jnp.concatenate([goal, goal], axis=1)
    diagonal = (iota((8, 256), 1) & 7) == iota((8, 256), 0)
    low_half = (iota((8, 256), 1) & 15) < 8

    first_ring(1)
    first_ring(3)
    from_partner(0)
    relay(0, 0)
    first_ring(2, (0,))
    from_partner(1)
    from_partner(3)
    from_partner(2, (0,))

    def tile(rel, dz):
        source = irrep ^ rel
        second = source ^ irrep ^ cd
        at = lax.rem(ring + dz, 4)
        first = source * GROUP + at * 2
        weights = jnp.concatenate(
            [panels[half, pl.ds(first, 2)].reshape(256, 128) for half in range(2)], axis=1
        )
        first_c = pl.multiple_of(at * 2 * CB, 2 * CB)
        rows = ints[:, pl.ds(second * WIR, WIR), pl.ds(first_c, 2 * CB), :]
        left = jnp.concatenate([rows[:, :, :CB], rows[:, :, CB:]], axis=3)
        left = left.reshape(OWN * WIR * CB, 256)
        term = jnp.dot(left, weights, preferred_element_type=F32)
        term = term.reshape(OWN * WIR, 2, 8, 256)
        acc[second] += jnp.where(low_half[None], term[:, 0], term[:, 1])

    relay(1, 0)
    relay(3, 0)
    relay(0, 1)
    first_ring(2, (1,))
    from_partner(2, (1,))
    for i in range(1, 4):
        pl.semaphore_signal(token, inc=1, device_id=(ab, cd ^ i), device_id_type=MESH)
    relay(2, 0, (0,))
    relay(1, 1)
    relay(3, 1)
    fetch.wait()
    rest_arrived(0, 0)
    rest_arrived(0, 1)
    for rel, dz in ((0, 0), (0, 1), (0, 3), (1, 0), (3, 0)):
        tile(rel, dz)
    relay(2, 0, (1,))
    for du in (1, 3):
        for dy in range(2):
            rest_arrived(du, dy)
    for rel, dz in ((1, 1), (1, 3), (3, 1), (3, 3)):
        tile(rel, dz)

    to_core = lax.rem(irrep, 2)

    def pass_copy(n, peer):
        return pltpu.make_async_remote_copy(
            src_ref=given.at[n],
            dst_ref=taken.at[n],
            send_sem=pass_send.at[n],
            recv_sem=pass_recv.at[n],
            device_id=(ab, peer),
            device_id_type=MESH,
        )

    my_tile = (irrep // 2 * 2 + high) * GROUP + slot

    def msg_copy(block, to_high):
        return pltpu.make_async_remote_copy(
            src_ref=msgs.at[block],
            dst_ref=mirror.at[my_tile],
            send_sem=msg_send,
            recv_sem=msg_recv,
            device_id=(block, to_high * 2 + to_core),
            device_id_type=MESH,
        )

    def local_copy():
        return pltpu.make_async_copy(msgs.at[ab], mirror.at[my_tile], msg_recv)

    def own_copy(n, peer, sender):
        return pltpu.make_async_remote_copy(
            src_ref=own.at[sender, n],
            dst_ref=own.at[sender, n],
            send_sem=own_send.at[n],
            recv_sem=own_recv.at[n],
            device_id=(ab, peer),
            device_id_type=MESH,
        )

    def half_copy(peer, sender):
        return pltpu.make_async_remote_copy(
            src_ref=halves.at[sender],
            dst_ref=halves.at[sender],
            send_sem=half_send,
            recv_sem=half_recv,
            device_id=(ab, peer),
            device_id_type=MESH,
        )

    def ending(*rels):
        folded = [
            jnp.sum(jnp.where(diagonal[None], acc[rel ^ cd], 0.0), axis=1) for rel in rels
        ]
        values = jnp.dot(
            split2(jnp.concatenate(folded, axis=0), 1),
            spread_pairs[...],
            preferred_element_type=F32,
        )
        kept = []
        for n in range(len(rels)):
            part = values[n * 72 : (n + 1) * 72]
            kept.append(jnp.concatenate([part, part], axis=0) * keep_rows[...])
        return jnp.dot(
            gather_rows[...], split2(jnp.concatenate(kept, axis=1), 0), preferred_element_type=F32
        )

    def finish(rel):
        second = rel ^ cd
        placed = ending(rel)
        pass_copy(rel // 2, other).wait_recv()
        placed = placed + taken[rel // 2]
        msgs[pl.ds(second * GROUP, GROUP)] = placed[16:].reshape(GROUP, 8, 128)
        for dz in (2, 1, 3, 0):
            for dy in (1, 0):
                for to_high in (1 - high, high):
                    block = second * GROUP + along_z[dz] + along_y[dy]
                    if dz or dy or to_high is not high:
                        msg_copy(block, to_high).start()
                        continue
                    here = (block == ab) & (to_core == core)
                    pl.when(~here)(msg_copy(block, to_high).start)
                    pl.when(here)(local_copy().start)

        at = second // 2
        own[high, at] = placed[:16].reshape(2, 8, 128)
        own_copy(at, cd ^ 2, high).start()

    far_arrived(1, 0)
    rest_arrived(2, 0, (0,))
    for dv in (1, 3):
        arrived(0, 2, dv, 1)
    far_arrived(1, 1)
    far_arrived(1, 3)
    for rel, dz in ((1, 2), (3, 2), (0, 2)):
        tile(rel, dz)
    passed = ending(1, 3)
    for n in range(2):
        given[n] = passed[:, n * 128 : (n + 1) * 128]
        pass_copy(n, other).start()
    rest_arrived(2, 0, (1,))
    for dv in (1, 3):
        arrived(1, 2, dv, 1)
    for du in (0, 1, 3):
        far_arrived(0, du)
    for dz in (0, 1, 3):
        tile(2, dz)
    pl.semaphore_wait(token, 3)
    finish(0)
    far_arrived(0, 2)
    far_arrived(1, 2)
    tile(2, 2)
    finish(2)

    def sent_items(i, carry):
        item_copy(i, 0, ab, ab).wait_send()
        return carry

    lax.fori_loop(0, len(sent), sent_items, 0)
    for n in range(2):
        pass_copy(n, cd).wait_send()

    pltpu.make_async_copy(msgs, mirror, msg_recv).wait()
    mirrored = jnp.sum(mirror[...].reshape(2, 2, 2, 4, 8, 128), axis=(1, 3))
    for n in range(2):
        own_copy(n, cd, 1 - high).wait_recv()
    halves[core] = (own[0] + own[1]) + mirrored
    half_copy(other, core).start()
    for n in range(2):
        own_copy(n, cd, high).wait_send()
    half_copy(cd, 1 - core).wait_recv()
    for second in range(IRREPS):
        out[second] = halves[second % 2, second // 2]
    half_copy(cd, core).wait_send()
    tiles = pltpu.make_async_copy(msgs.at[pl.ds(0, 31)], mirror.at[pl.ds(0, 31)], msg_send)
    tiles.wait()

    @pl.when(to_core != core)
    def _():
        pltpu.make_async_copy(msgs.at[0], mirror.at[0], msg_send).wait()


def on_device(integrals, amplitudes, block_sizes):
    vmem = pl.BlockSpec(memory_space=pltpu.VMEM)
    packed = pl.pallas_call(
        kernel,
        out_shape=jax.ShapeDtypeStruct((IRREPS, 2, 8, 128), F32),
        in_specs=[
            pl.BlockSpec(memory_space=pltpu.SMEM),
            pl.BlockSpec(memory_space=pl.ANY),
            pl.BlockSpec(memory_space=pl.ANY),
        ],
        out_specs=vmem,
        scratch_shapes=[
            pltpu.VMEM(integrals.shape, BF16),
            pltpu.VMEM(amplitudes.shape, BF16),
            pltpu.VMEM((2, 32, BLK, NPAIR * CB // 2), BF16),
            pltpu.VMEM((IRREPS, OWN * WIR, 8, 256), F32),
            pltpu.VMEM((2, 80, 128), F32),
            pltpu.VMEM((2, 80, 128), F32),
            pltpu.VMEM((32, 8, 128), F32),
            pltpu.VMEM((32, 8, 128), F32),
            pltpu.VMEM((2, 2, 2, 8, 128), F32),
            pltpu.VMEM((2, 2, 2, 8, 128), F32),
            pltpu.VMEM((512, 128), BF16),
            pltpu.VMEM((144, 128), F32),
            pltpu.VMEM((80, 288), BF16),
            pltpu.SemaphoreType.DMA,
            pltpu.SemaphoreType.DMA,
            pltpu.SemaphoreType.DMA((62,)),
            pltpu.SemaphoreType.DMA((2, 32)),
            pltpu.SemaphoreType.DMA((2,)),
            pltpu.SemaphoreType.DMA((2,)),
            pltpu.SemaphoreType.DMA,
            pltpu.SemaphoreType.DMA,
            pltpu.SemaphoreType.DMA((2,)),
            pltpu.SemaphoreType.DMA((2,)),
            pltpu.SemaphoreType.DMA,
            pltpu.SemaphoreType.DMA,
            pltpu.SemaphoreType.REGULAR,
        ],
        compiler_params=pltpu.CompilerParams(
            collective_id=0, has_side_effects=True, vmem_limit_bytes=56 << 20
        ),
        name="ladder",
    )(block_sizes, amplitudes, integrals)
    packed = packed.reshape(IRREPS, 2, 2, 4, 2, 4, NPAIR)[:, :, :, :OWN, :, :OWN]
    return packed.transpose(6, 3, 0, 1, 2, 4, 5).reshape(NPAIR, OWN, IRREPS * WIR)


def solution(mesh):
    placed = (P("ab", None, None, "cd"), P(None, "ab", "cd"), P())
    return jax.shard_map(
        on_device, mesh=mesh, in_specs=placed, out_specs=P(None, "ab", None), check_vma=False
    )
```

```python
import jax
import jax.numpy as jnp
from jax import lax
from jax.experimental import pallas as pl
from jax.experimental.pallas import tpu as pltpu
from jax.sharding import PartitionSpec as P

IRREPS = 4
BLK = 128
NPAIR = 16
WIR = 24
GROUP = 8
OWN = 3
CB = 16
MESH = pl.DeviceIdType.MESH
F32 = jnp.float32
BF16 = jnp.bfloat16


def iota(shape, dim):
    return lax.broadcasted_iota(jnp.int32, shape, dim)


def split2(x, axis):
    high = x.astype(BF16)
    low = (x - high.astype(F32)).astype(BF16)
    return jnp.concatenate([high, low], axis=axis)


def kernel(
    sizes_at, amps, integrals, out, sizes, ints, plain, panels, acc, given, taken, msgs, mirror, own, halves,
    spread_pairs, keep_rows, gather_rows, take_lanes, put_rows, keep_lanes,
    sizes_sem, ints_sem, plain_sem, send_sem, item_recv, pass_send, pass_recv,
    msg_send, msg_recv, own_send, own_recv, half_send, half_recv, token,
):
    ab = lax.axis_index("ab")
    cd = lax.axis_index("cd")
    irrep = ab // GROUP
    slot = lax.rem(ab, GROUP)
    slot_low = lax.rem(slot // 2, 2)
    slot_lane = lax.rem(slot, 2)
    ring = slot // 2
    pick = slot_lane
    core = lax.rem(cd, 2)
    high = cd // 2
    other = cd ^ 1

    fetch_own = pltpu.make_async_copy(amps, plain, plain_sem)
    fetch_own.start()
    fetch_sizes = pltpu.make_async_copy(sizes_at, sizes, sizes_sem)
    fetch_sizes.start()

    along_x = [lax.rem(irrep + d, 4) * GROUP for d in range(4)]
    along_z = [lax.rem(ring + d, 4) * 2 for d in range(4)]
    along_y = [pick, 1 - pick]

    def place(half, du, dv, dy):
        if half == 0:
            return along_x[dv] + along_z[du] + along_y[dy]
        return along_x[du] + along_z[dv] + along_y[dy]

    barrier = pltpu.get_barrier_semaphore()
    for du, dv, dy in ((1, 0, 0), (3, 0, 0), (2, 0, 0), (0, 1, 0), (0, 3, 0), (0, 2, 0), (0, 0, 1)):
        pl.semaphore_signal(
            barrier, inc=1, device_id=(place(0, du, dv, dy), cd), device_id_type=MESH
        )
    for i in range(1, 4):
        pl.semaphore_signal(barrier, inc=1, device_id=(ab, cd ^ i), device_id_type=MESH)

    fetch = pltpu.make_async_copy(integrals, ints, ints_sem)
    fetch.start()

    fetch_sizes.wait()
    row_limit = sizes[irrep] - slot * CB
    col_limit = sizes[cd]
    shape = (NPAIR * CB, BLK)
    keep = ((iota(shape, 0) & (CB - 1)) < row_limit) & (iota(shape, 1) < col_limit)
    fetch_own.wait()
    turned = jnp.where(keep, plain[...].reshape(shape).astype(F32), 0.0).T.astype(BF16)
    panels[0, ab] = turned[:, :128]
    panels[1, ab] = turned[:, 128:]

    def item_copy(i, half, peer, block):
        return pltpu.make_async_remote_copy(
            src_ref=panels.at[half, block],
            dst_ref=panels.at[half, block],
            send_sem=send_sem.at[i],
            recv_sem=item_recv.at[half, block],
            device_id=(peer, cd),
            device_id_type=MESH,
        )

    sent = []

    def send(half, block, to):
        item_copy(len(sent), half, place(half, *to), place(half, *block)).start()
        sent.append(half)

    def arrived(half, *block):
        item_copy(0, half, ab, place(half, *block)).wait_recv()

    def onward(half, du, dy):
        send(half, (du, 0, dy), (0, 1, 0))
        send(half, (du, 0, dy), (0, 3, 0))
        if (du, dy) == (2, 1):
            send(half, (du, 0, dy), (0, 2, 0))

    both = (0, 1)

    def first_ring(du, halves=both):
        for half in halves:
            arrived(half, du, 0, 0)
            send(half, (du, 0, 0), (0, 0, 1))
            onward(half, du, 0)

    def from_partner(du, halves=both):
        for half in halves:
            arrived(half, du, 0, 1)
            onward(half, du, 1)

    from_below = ((0, 0), (2, 0), (1, 1), (3, 1))

    def relay(du, dy, halves=both):
        dv = 3 if (du, dy) in from_below else 1
        for half in halves:
            arrived(half, du, dv, dy)
            send(half, (du, dv, dy), (0, 4 - dv, 0))

    def rest_arrived(du, dy, halves=both):
        dv = 1 if (du, dy) in from_below else 3
        for half in halves:
            arrived(half, du, dv, dy)

    def far_arrived(half, du):
        for dy in range(2):
            arrived(half, du, 2, dy)

    pl.semaphore_wait(barrier, 10)

    for du in (1, 3):
        for half in range(2):
            send(half, (0, 0, 0), (du, 0, 0))
    for half in range(2):
        onward(half, 0, 0)
    for half in range(2):
        send(half, (0, 0, 0), (0, 0, 1))
    for half in range(2):
        send(half, (0, 0, 0), (2, 0, 0))

    spread_pairs[...] = (
        (iota((512, 128), 1) & 15) == ((iota((512, 128), 0) & 255) >> 4)
    ).astype(BF16)
    lane = iota((72, 128), 1)
    lane_slot, lane_item = lane >> 6, (lane >> 4) & 3
    row_a, row_b = iota((72, 128), 0) // WIR, lax.rem(iota((72, 128), 0), WIR)
    own_row = (lane_slot == ((row_b // OWN) & 1)) & (lane_item == lax.rem(row_b, OWN))
    keep_rows[pl.ds(0, 72)] = own_row.astype(F32)
    keep_rows[pl.ds(72, 72)] = ((lane_slot == slot_lane) & (lane_item == row_a)).astype(F32)
    frm = iota((80, 144), 1)
    frm_row = lax.rem(frm, 72)
    frm_a, frm_b = frm_row // WIR, lax.rem(frm_row, WIR)
    frm_slot, frm_k = frm_b // OWN, lax.rem(frm_b, OWN)
    goal = jnp.where(
        frm < 72,
        (frm_slot >> 2) * 8 + ((frm_slot >> 1) & 1) * 4 + frm_a,
        16 + frm_slot * 8 + slot_low * 4 + frm_k,
    )
    goal = (iota((80, 144), 0) == goal).astype(BF16)
    gather_rows[...] = jnp.concatenate([goal, goal], axis=1)
    frm = iota((96, 128), 0)
    take_lanes[...] = (
        iota((96, 128), 1) == (frm // 48) * 64 + (lax.rem(frm, 48) >> 4) * 16 + (frm & 15)
    ).astype(BF16)
    for a in range(OWN):
        b = iota((64, 128), 1)
        b_row = lax.rem(b, WIR) // 6
        b_row = (b // (2 * WIR)) * 16 + (b_row >> 1) * 8 + (b_row & 1) * 4 + a
        b_here = (((b // WIR) & 1) == core) & (b < IRREPS * WIR)
        put_rows[:, pl.ds(a * 128, 128)] = (
            ((iota((64, 128), 0) & 31) == b_row) & b_here
        ).astype(BF16)
    frm = iota((96, 128), 0)
    keep_lanes[...] = ((frm >> 4) == lax.rem(iota((96, 128), 1), 6)).astype(F32)
    diagonal = (iota((8, 256), 1) & 7) == iota((8, 256), 0)
    low_half = (iota((8, 256), 1) & 15) < 8

    def tile(rel, dz):
        source = irrep ^ rel
        second = source ^ irrep ^ cd
        at = lax.rem(ring + dz, 4)
        first = source * GROUP + at * 2
        weights = jnp.concatenate(
            [panels[half, pl.ds(first, 2)].reshape(256, 128) for half in range(2)], axis=1
        )
        first_c = pl.multiple_of(at * 2 * CB, 2 * CB)
        rows = ints[:, pl.ds(second * WIR, WIR), pl.ds(first_c, 2 * CB), :]
        left = jnp.concatenate([rows[:, :, :CB], rows[:, :, CB:]], axis=3)
        left = left.reshape(OWN * WIR * CB, 256)
        term = jnp.dot(left, weights, preferred_element_type=F32)
        term = term.reshape(OWN * WIR, 2, 8, 256)
        term = jnp.where(low_half[None], term[:, 0], term[:, 1])
        if dz:
            term = acc[second] + term
        acc[second] = term

    first_ring(1)
    first_ring(3)
    from_partner(0)
    relay(0, 0)
    first_ring(2)
    from_partner(1)
    from_partner(3)
    fetch.wait()
    relay(1, 0)
    relay(3, 0)
    relay(0, 1)
    from_partner(2)
    for i in range(1, 4):
        pl.semaphore_signal(token, inc=1, device_id=(ab, cd ^ i), device_id_type=MESH)
    relay(2, 0)
    relay(1, 1)
    relay(3, 1)
    rest_arrived(0, 0)
    rest_arrived(0, 1)
    for rel, dz in ((0, 0), (0, 1), (0, 3), (1, 0), (3, 0)):
        tile(rel, dz)
    for du in (1, 3):
        for dy in range(2):
            rest_arrived(du, dy)
    for rel, dz in ((1, 1), (1, 3), (3, 1), (3, 3)):
        tile(rel, dz)

    to_core = lax.rem(irrep, 2)

    def pass_copy(n, peer):
        return pltpu.make_async_remote_copy(
            src_ref=given.at[n],
            dst_ref=taken.at[n],
            send_sem=pass_send.at[n],
            recv_sem=pass_recv.at[n],
            device_id=(ab, peer),
            device_id_type=MESH,
        )

    my_tile = (irrep // 2 * 2 + high) * GROUP + slot

    def msg_copy(block, to_high):
        return pltpu.make_async_remote_copy(
            src_ref=msgs.at[block],
            dst_ref=mirror.at[my_tile],
            send_sem=msg_send,
            recv_sem=msg_recv,
            device_id=(block, to_high * 2 + to_core),
            device_id_type=MESH,
        )

    def local_copy():
        return pltpu.make_async_copy(msgs.at[ab], mirror.at[my_tile], msg_recv)

    def own_copy(n, peer, sender):
        return pltpu.make_async_remote_copy(
            src_ref=own.at[sender, n],
            dst_ref=own.at[sender, n],
            send_sem=own_send.at[n],
            recv_sem=own_recv.at[n],
            device_id=(ab, peer),
            device_id_type=MESH,
        )

    def half_copy(peer, sender):
        return pltpu.make_async_remote_copy(
            src_ref=halves.at[sender],
            dst_ref=halves.at[sender],
            send_sem=half_send,
            recv_sem=half_recv,
            device_id=(ab, peer),
            device_id_type=MESH,
        )

    def ending(*rels):
        folded = [
            jnp.sum(jnp.where(diagonal[None], acc[rel ^ cd], 0.0), axis=1) for rel in rels
        ]
        values = jnp.dot(
            split2(jnp.concatenate(folded, axis=0), 1),
            spread_pairs[...],
            preferred_element_type=F32,
        )
        kept = []
        for n in range(len(rels)):
            part = values[n * 72 : (n + 1) * 72]
            kept.append(jnp.concatenate([part, part], axis=0) * keep_rows[...])
        return jnp.dot(
            gather_rows[...], split2(jnp.concatenate(kept, axis=1), 0), preferred_element_type=F32
        )

    def finish(rel, placed):
        second = rel ^ cd
        pass_copy(rel // 2, other).wait_recv()
        placed = placed + taken[rel // 2]
        msgs[pl.ds(second * GROUP, GROUP)] = placed[16:].reshape(GROUP, 8, 128)
        for dz in (2, 1, 3, 0):
            for dy in (1, 0):
                for to_high in (1 - high, high):
                    block = second * GROUP + along_z[dz] + along_y[dy]
                    if dz or dy or to_high is not high:
                        msg_copy(block, to_high).start()
                        continue
                    here = (block == ab) & (to_core == core)
                    pl.when(~here)(msg_copy(block, to_high).start)
                    pl.when(here)(local_copy().start)

        at = second // 2
        own[high, at] = placed[:16].reshape(2, 8, 128)
        own_copy(at, cd ^ 2, high).start()

    far_arrived(1, 0)
    rest_arrived(2, 0, (0,))
    for dv in (1, 3):
        arrived(0, 2, dv, 1)
    far_arrived(1, 1)
    far_arrived(1, 3)
    for rel, dz in ((1, 2), (3, 2), (0, 2)):
        tile(rel, dz)
    passed = ending(1, 3)
    for n in range(2):
        given[n] = passed[:, n * 128 : (n + 1) * 128]
        pass_copy(n, other).start()
    rest_arrived(2, 0, (1,))
    for dv in (1, 3):
        arrived(1, 2, dv, 1)
    for du in (0, 1, 3):
        far_arrived(0, du)
    for dz in (0, 1, 3):
        tile(2, dz)
    far_arrived(0, 2)
    far_arrived(1, 2)
    tile(2, 2)
    pl.semaphore_wait(token, 3)
    placed = ending(2, 0)
    finish(2, placed[:, :128])
    finish(0, placed[:, 128:])

    def sent_items(i, carry):
        item_copy(i, 0, ab, ab).wait_send()
        return carry

    lax.fori_loop(0, len(sent), sent_items, 0)
    for n in range(2):
        pass_copy(n, cd).wait_send()

    pltpu.make_async_copy(msgs, mirror, msg_recv).wait()
    mirrored = jnp.sum(mirror[...].reshape(2, 2, 2, 4, 8, 128), axis=(1, 3))
    for n in range(2):
        own_copy(n, cd, 1 - high).wait_recv()
    total = ((own[0] + own[1]) + mirrored).reshape(32, 128)
    turned = lax.dot_general(
        take_lanes[...], split2(total, 0), (((1,), (1,)), ((), ())), preferred_element_type=F32
    )
    wide = jnp.dot(turned.astype(BF16), put_rows[...], preferred_element_type=F32)
    for a in range(OWN):
        part = wide[:, a * 128 : (a + 1) * 128] * keep_lanes[...]
        halves[core, a] = jnp.sum(part.reshape(6, NPAIR, 128), axis=0)
    half_copy(other, core).start()
    for n in range(2):
        own_copy(n, cd, high).wait_send()
    half_copy(cd, 1 - core).wait_recv()
    out[...] = (halves[0] + halves[1])[:, :, : IRREPS * WIR]
    half_copy(cd, core).wait_send()
    tiles = pltpu.make_async_copy(msgs.at[pl.ds(0, 31)], mirror.at[pl.ds(0, 31)], msg_send)
    tiles.wait()

    @pl.when(to_core != core)
    def _():
        pltpu.make_async_copy(msgs.at[0], mirror.at[0], msg_send).wait()


def on_device(integrals, amplitudes, block_sizes):
    vmem = pl.BlockSpec(memory_space=pltpu.VMEM)
    rows = pl.pallas_call(
        kernel,
        out_shape=jax.ShapeDtypeStruct((OWN, NPAIR, IRREPS * WIR), F32),
        in_specs=[
            pl.BlockSpec(memory_space=pltpu.HBM),
            pl.BlockSpec(memory_space=pltpu.HBM),
            pl.BlockSpec(memory_space=pltpu.HBM),
        ],
        out_specs=vmem,
        scratch_shapes=[
            pltpu.SMEM((IRREPS,), jnp.int32),
            pltpu.VMEM(integrals.shape, BF16),
            pltpu.VMEM(amplitudes.shape, BF16),
            pltpu.VMEM((2, 32, BLK, NPAIR * CB // 2), BF16),
            pltpu.VMEM((IRREPS, OWN * WIR, 8, 256), F32),
            pltpu.VMEM((2, 80, 128), F32),
            pltpu.VMEM((2, 80, 128), F32),
            pltpu.VMEM((32, 8, 128), F32),
            pltpu.VMEM((32, 8, 128), F32),
            pltpu.VMEM((2, 2, 2, 8, 128), F32),
            pltpu.VMEM((2, OWN, NPAIR, 128), F32),
            pltpu.VMEM((512, 128), BF16),
            pltpu.VMEM((144, 128), F32),
            pltpu.VMEM((80, 288), BF16),
            pltpu.VMEM((96, 128), BF16),
            pltpu.VMEM((64, OWN * 128), BF16),
            pltpu.VMEM((96, 128), F32),
            pltpu.SemaphoreType.DMA,
            pltpu.SemaphoreType.DMA,
            pltpu.SemaphoreType.DMA,
            pltpu.SemaphoreType.DMA((62,)),
            pltpu.SemaphoreType.DMA((2, 32)),
            pltpu.SemaphoreType.DMA((2,)),
            pltpu.SemaphoreType.DMA((2,)),
            pltpu.SemaphoreType.DMA,
            pltpu.SemaphoreType.DMA,
            pltpu.SemaphoreType.DMA((2,)),
            pltpu.SemaphoreType.DMA((2,)),
            pltpu.SemaphoreType.DMA,
            pltpu.SemaphoreType.DMA,
            pltpu.SemaphoreType.REGULAR,
        ],
        compiler_params=pltpu.CompilerParams(
            collective_id=0, has_side_effects=True, vmem_limit_bytes=56 << 20
        ),
        name="ladder",
    )(block_sizes, amplitudes, integrals)
    return rows.transpose(1, 0, 2)


def solution(mesh):
    placed = (P("ab", None, None, "cd"), P(None, "ab", "cd"), P())
    return jax.shard_map(
        on_device, mesh=mesh, in_specs=placed, out_specs=P(None, "ab", None), check_vma=False
    )
```

```python
import jax
import jax.numpy as jnp
from jax import lax
from jax.experimental import pallas as pl
from jax.experimental.pallas import tpu as pltpu
from jax.sharding import PartitionSpec as P

IRREPS = 4
BLK = 128
NPAIR = 16
WIR = 24
GROUP = 8
OWN = 3
CB = 16
MESH = pl.DeviceIdType.MESH
F32 = jnp.float32
BF16 = jnp.bfloat16


def iota(shape, dim):
    return lax.broadcasted_iota(jnp.int32, shape, dim)


def split2(x, axis):
    high = x.astype(BF16)
    low = (x - high.astype(F32)).astype(BF16)
    return jnp.concatenate([high, low], axis=axis)


def kernel(
    sizes_at, amps, integrals, out, sizes, ints, plain, panels, acc, given, taken, msgs, mirror, own, halves,
    spread_pairs, keep_rows, gather_rows, take_lanes, put_rows, keep_lanes,
    sizes_sem, ints_sem, plain_sem, send_sem, item_recv, pass_send, pass_recv,
    msg_send, msg_recv, own_send, own_recv, half_send, half_recv, token,
):
    ab = lax.axis_index("ab")
    cd = lax.axis_index("cd")
    irrep = ab // GROUP
    slot = lax.rem(ab, GROUP)
    slot_low = lax.rem(slot // 2, 2)
    slot_lane = lax.rem(slot, 2)
    ring = slot // 2
    pick = slot_lane
    core = lax.rem(cd, 2)
    high = cd // 2
    other = cd ^ 1

    fetch_own = pltpu.make_async_copy(amps, plain, plain_sem)
    fetch_own.start()
    fetch_sizes = pltpu.make_async_copy(sizes_at, sizes, sizes_sem)
    fetch_sizes.start()

    along_x = [lax.rem(irrep + d, 4) * GROUP for d in range(4)]
    along_z = [lax.rem(ring + d, 4) * 2 for d in range(4)]
    along_y = [pick, 1 - pick]

    def place(half, du, dv, dy):
        if half == 0:
            return along_x[dv] + along_z[du] + along_y[dy]
        return along_x[du] + along_z[dv] + along_y[dy]

    barrier = pltpu.get_barrier_semaphore()
    for du, dv, dy in ((1, 0, 0), (3, 0, 0), (2, 0, 0), (0, 1, 0), (0, 3, 0), (0, 2, 0), (0, 0, 1)):
        pl.semaphore_signal(
            barrier, inc=1, device_id=(place(0, du, dv, dy), cd), device_id_type=MESH
        )
    for i in range(1, 4):
        pl.semaphore_signal(barrier, inc=1, device_id=(ab, cd ^ i), device_id_type=MESH)

    fetch = pltpu.make_async_copy(integrals, ints, ints_sem)
    fetch.start()

    fetch_sizes.wait()
    row_limit = sizes[irrep] - slot * CB
    col_limit = sizes[cd]
    shape = (NPAIR * CB, BLK)
    keep = ((iota(shape, 0) & (CB - 1)) < row_limit) & (iota(shape, 1) < col_limit)
    fetch_own.wait()
    turned = jnp.where(keep, plain[...].reshape(shape).astype(F32), 0.0).T.astype(BF16)
    panels[0, ab] = turned[:, :128]
    panels[1, ab] = turned[:, 128:]

    def item_copy(i, half, peer, block):
        return pltpu.make_async_remote_copy(
            src_ref=panels.at[half, block],
            dst_ref=panels.at[half, block],
            send_sem=send_sem.at[i],
            recv_sem=item_recv.at[half, block],
            device_id=(peer, cd),
            device_id_type=MESH,
        )

    sent = []

    def send(half, block, to):
        item_copy(len(sent), half, place(half, *to), place(half, *block)).start()
        sent.append(half)

    def arrived(half, *block):
        item_copy(0, half, ab, place(half, *block)).wait_recv()

    def onward(half, du, dy):
        send(half, (du, 0, dy), (0, 1, 0))
        send(half, (du, 0, dy), (0, 3, 0))
        if (du, dy) == (2, 1):
            send(half, (du, 0, dy), (0, 2, 0))

    both = (0, 1)

    def first_ring(du, halves=both):
        for half in halves:
            arrived(half, du, 0, 0)
            send(half, (du, 0, 0), (0, 0, 1))
            onward(half, du, 0)

    def from_partner(du, halves=both):
        for half in halves:
            arrived(half, du, 0, 1)
            onward(half, du, 1)

    from_below = ((0, 0), (1, 0), (3, 1))

    def relay(du, dy, halves=both):
        dv = 3 if (du, dy) in from_below else 1
        for half in halves:
            arrived(half, du, dv, dy)
            send(half, (du, dv, dy), (0, 4 - dv, 0))

    def rest_arrived(du, dy, halves=both):
        dv = 1 if (du, dy) in from_below else 3
        for half in halves:
            arrived(half, du, dv, dy)

    def far_to_partner(du):
        for half in range(2):
            arrived(half, du, 2, 0)
            send(half, (du, 2, 0), (0, 0, 1))

    def far_arrived(half, du):
        for dy in range(1 if du == 0 else 0, 2):
            arrived(half, du, 2, dy)

    pl.semaphore_wait(barrier, 10)

    for du in (1, 3):
        for half in range(2):
            send(half, (0, 0, 0), (du, 0, 0))
    for half in range(2):
        onward(half, 0, 0)
    for half in range(2):
        send(half, (0, 0, 0), (0, 0, 1))
    for half in range(2):
        send(half, (0, 0, 0), (2, 0, 0))

    spread_pairs[...] = (
        (iota((512, 128), 1) & 15) == ((iota((512, 128), 0) & 255) >> 4)
    ).astype(BF16)
    lane = iota((72, 128), 1)
    lane_slot, lane_item = lane >> 6, (lane >> 4) & 3
    row_a, row_b = iota((72, 128), 0) // WIR, lax.rem(iota((72, 128), 0), WIR)
    own_row = (lane_slot == ((row_b // OWN) & 1)) & (lane_item == lax.rem(row_b, OWN))
    keep_rows[pl.ds(0, 72)] = own_row.astype(F32)
    keep_rows[pl.ds(72, 72)] = ((lane_slot == slot_lane) & (lane_item == row_a)).astype(F32)
    frm = iota((80, 144), 1)
    frm_row = lax.rem(frm, 72)
    frm_a, frm_b = frm_row // WIR, lax.rem(frm_row, WIR)
    frm_slot, frm_k = frm_b // OWN, lax.rem(frm_b, OWN)
    goal = jnp.where(
        frm < 72,
        (frm_slot >> 2) * 8 + ((frm_slot >> 1) & 1) * 4 + frm_a,
        16 + frm_slot * 8 + slot_low * 4 + frm_k,
    )
    goal = (iota((80, 144), 0) == goal).astype(BF16)
    gather_rows[...] = jnp.concatenate([goal, goal], axis=1)
    frm = iota((96, 128), 0)
    take_lanes[...] = (
        iota((96, 128), 1) == (frm // 48) * 64 + (lax.rem(frm, 48) >> 4) * 16 + (frm & 15)
    ).astype(BF16)
    for a in range(OWN):
        b = iota((64, 128), 1)
        b_row = lax.rem(b, WIR) // 6
        b_row = (b // (2 * WIR)) * 16 + (b_row >> 1) * 8 + (b_row & 1) * 4 + a
        b_here = (((b // WIR) & 1) == core) & (b < IRREPS * WIR)
        put_rows[:, pl.ds(a * 128, 128)] = (
            ((iota((64, 128), 0) & 31) == b_row) & b_here
        ).astype(BF16)
    frm = iota((96, 128), 0)
    keep_lanes[...] = ((frm >> 4) == lax.rem(iota((96, 128), 1), 6)).astype(F32)
    diagonal = (iota((8, 256), 1) & 7) == iota((8, 256), 0)
    low_half = (iota((8, 256), 1) & 15) < 8

    def tile(rel, dz):
        source = irrep ^ rel
        second = source ^ irrep ^ cd
        at = lax.rem(ring + dz, 4)
        first = source * GROUP + at * 2
        weights = jnp.concatenate(
            [panels[half, pl.ds(first, 2)].reshape(256, 128) for half in range(2)], axis=1
        )
        first_c = pl.multiple_of(at * 2 * CB, 2 * CB)
        rows = ints[:, pl.ds(second * WIR, WIR), pl.ds(first_c, 2 * CB), :]
        left = jnp.concatenate([rows[:, :, :CB], rows[:, :, CB:]], axis=3)
        left = left.reshape(OWN * WIR * CB, 256)
        term = jnp.dot(left, weights, preferred_element_type=F32)
        term = term.reshape(OWN * WIR, 2, 8, 256)
        term = jnp.where(low_half[None], term[:, 0], term[:, 1])
        if dz:
            term = acc[second] + term
        acc[second] = term

    first_ring(1)
    first_ring(3)
    from_partner(0)
    relay(0, 0)
    first_ring(2)
    from_partner(1)
    from_partner(3)
    fetch.wait()
    relay(1, 0)
    relay(3, 0)
    from_partner(2)
    for i in range(1, 4):
        pl.semaphore_signal(token, inc=1, device_id=(ab, cd ^ i), device_id_type=MESH)
    relay(2, 0)
    relay(1, 1)
    relay(3, 1)
    far_to_partner(0)
    rest_arrived(0, 0)
    for half in range(2):
        arrived(half, 0, 1, 1)
        arrived(half, 0, 3, 1)
    for rel, dz in ((0, 0), (0, 1), (0, 3), (1, 0), (3, 0)):
        tile(rel, dz)
    for du in (1, 3):
        for dy in range(2):
            rest_arrived(du, dy)
    for rel, dz in ((1, 1), (1, 3), (3, 1), (3, 3)):
        tile(rel, dz)

    to_core = lax.rem(irrep, 2)

    def pass_copy(n, peer):
        return pltpu.make_async_remote_copy(
            src_ref=given.at[n],
            dst_ref=taken.at[n],
            send_sem=pass_send.at[n],
            recv_sem=pass_recv.at[n],
            device_id=(ab, peer),
            device_id_type=MESH,
        )

    my_tile = (irrep // 2 * 2 + high) * GROUP + slot

    def msg_copy(block, to_high):
        return pltpu.make_async_remote_copy(
            src_ref=msgs.at[block],
            dst_ref=mirror.at[my_tile],
            send_sem=msg_send,
            recv_sem=msg_recv,
            device_id=(block, to_high * 2 + to_core),
            device_id_type=MESH,
        )

    def local_copy():
        return pltpu.make_async_copy(msgs.at[ab], mirror.at[my_tile], msg_recv)

    def own_copy(n, peer, sender):
        return pltpu.make_async_remote_copy(
            src_ref=own.at[sender, n],
            dst_ref=own.at[sender, n],
            send_sem=own_send.at[n],
            recv_sem=own_recv.at[n],
            device_id=(ab, peer),
            device_id_type=MESH,
        )

    def half_copy(peer, sender):
        return pltpu.make_async_remote_copy(
            src_ref=halves.at[sender],
            dst_ref=halves.at[sender],
            send_sem=half_send,
            recv_sem=half_recv,
            device_id=(ab, peer),
            device_id_type=MESH,
        )

    def ending(*rels):
        folded = [
            jnp.sum(jnp.where(diagonal[None], acc[rel ^ cd], 0.0), axis=1) for rel in rels
        ]
        values = jnp.dot(
            split2(jnp.concatenate(folded, axis=0), 1),
            spread_pairs[...],
            preferred_element_type=F32,
        )
        kept = []
        for n in range(len(rels)):
            part = values[n * 72 : (n + 1) * 72]
            kept.append(jnp.concatenate([part, part], axis=0) * keep_rows[...])
        return jnp.dot(
            gather_rows[...], split2(jnp.concatenate(kept, axis=1), 0), preferred_element_type=F32
        )

    def finish(rel, placed):
        second = rel ^ cd
        pass_copy(rel // 2, other).wait_recv()
        placed = placed + taken[rel // 2]
        msgs[pl.ds(second * GROUP, GROUP)] = placed[16:].reshape(GROUP, 8, 128)
        for dz in (2, 1, 3, 0):
            for dy in (1, 0):
                for to_high in (1 - high, high):
                    block = second * GROUP + along_z[dz] + along_y[dy]
                    if dz or dy or to_high is not high:
                        msg_copy(block, to_high).start()
                        continue
                    here = (block == ab) & (to_core == core)
                    pl.when(~here)(msg_copy(block, to_high).start)
                    pl.when(here)(local_copy().start)

        at = second // 2
        own[high, at] = placed[:16].reshape(2, 8, 128)
        own_copy(at, cd ^ 2, high).start()

    far_arrived(1, 0)
    rest_arrived(2, 0, (0,))
    for dv in (1, 3):
        arrived(0, 2, dv, 1)
    far_arrived(1, 1)
    far_arrived(1, 3)
    for rel, dz in ((1, 2), (3, 2), (0, 2)):
        tile(rel, dz)
    passed = ending(1, 3)
    for n in range(2):
        given[n] = passed[:, n * 128 : (n + 1) * 128]
        pass_copy(n, other).start()
    rest_arrived(2, 0, (1,))
    for dv in (1, 3):
        arrived(1, 2, dv, 1)
    for du in (0, 1, 3):
        far_arrived(0, du)
    for dz in (0, 1, 3):
        tile(2, dz)
    far_arrived(0, 2)
    far_arrived(1, 2)
    tile(2, 2)
    pl.semaphore_wait(token, 3)
    placed = ending(2, 0)
    finish(2, placed[:, :128])
    finish(0, placed[:, 128:])

    def sent_items(i, carry):
        item_copy(i, 0, ab, ab).wait_send()
        return carry

    lax.fori_loop(0, len(sent), sent_items, 0)
    for n in range(2):
        pass_copy(n, cd).wait_send()

    pltpu.make_async_copy(msgs, mirror, msg_recv).wait()
    mirrored = jnp.sum(mirror[...].reshape(2, 2, 2, 4, 8, 128), axis=(1, 3))
    for n in range(2):
        own_copy(n, cd, 1 - high).wait_recv()
    total = ((own[0] + own[1]) + mirrored).reshape(32, 128)
    turned = lax.dot_general(
        take_lanes[...], split2(total, 0), (((1,), (1,)), ((), ())), preferred_element_type=F32
    )
    wide = jnp.dot(turned.astype(BF16), put_rows[...], preferred_element_type=F32)
    for a in range(OWN):
        part = wide[:, a * 128 : (a + 1) * 128] * keep_lanes[...]
        halves[core, a] = jnp.sum(part.reshape(6, NPAIR, 128), axis=0)
    half_copy(other, core).start()
    for n in range(2):
        own_copy(n, cd, high).wait_send()
    half_copy(cd, 1 - core).wait_recv()
    out[...] = (halves[0] + halves[1])[:, :, : IRREPS * WIR]
    half_copy(cd, core).wait_send()
    tiles = pltpu.make_async_copy(msgs.at[pl.ds(0, 31)], mirror.at[pl.ds(0, 31)], msg_send)
    tiles.wait()

    @pl.when(to_core != core)
    def _():
        pltpu.make_async_copy(msgs.at[0], mirror.at[0], msg_send).wait()


def on_device(integrals, amplitudes, block_sizes):
    vmem = pl.BlockSpec(memory_space=pltpu.VMEM)
    rows = pl.pallas_call(
        kernel,
        out_shape=jax.ShapeDtypeStruct((OWN, NPAIR, IRREPS * WIR), F32),
        in_specs=[
            pl.BlockSpec(memory_space=pltpu.HBM),
            pl.BlockSpec(memory_space=pltpu.HBM),
            pl.BlockSpec(memory_space=pltpu.HBM),
        ],
        out_specs=vmem,
        scratch_shapes=[
            pltpu.SMEM((IRREPS,), jnp.int32),
            pltpu.VMEM(integrals.shape, BF16),
            pltpu.VMEM(amplitudes.shape, BF16),
            pltpu.VMEM((2, 32, BLK, NPAIR * CB // 2), BF16),
            pltpu.VMEM((IRREPS, OWN * WIR, 8, 256), F32),
            pltpu.VMEM((2, 80, 128), F32),
            pltpu.VMEM((2, 80, 128), F32),
            pltpu.VMEM((32, 8, 128), F32),
            pltpu.VMEM((32, 8, 128), F32),
            pltpu.VMEM((2, 2, 2, 8, 128), F32),
            pltpu.VMEM((2, OWN, NPAIR, 128), F32),
            pltpu.VMEM((512, 128), BF16),
            pltpu.VMEM((144, 128), F32),
            pltpu.VMEM((80, 288), BF16),
            pltpu.VMEM((96, 128), BF16),
            pltpu.VMEM((64, OWN * 128), BF16),
            pltpu.VMEM((96, 128), F32),
            pltpu.SemaphoreType.DMA,
            pltpu.SemaphoreType.DMA,
            pltpu.SemaphoreType.DMA,
            pltpu.SemaphoreType.DMA((62,)),
            pltpu.SemaphoreType.DMA((2, 32)),
            pltpu.SemaphoreType.DMA((2,)),
            pltpu.SemaphoreType.DMA((2,)),
            pltpu.SemaphoreType.DMA,
            pltpu.SemaphoreType.DMA,
            pltpu.SemaphoreType.DMA((2,)),
            pltpu.SemaphoreType.DMA((2,)),
            pltpu.SemaphoreType.DMA,
            pltpu.SemaphoreType.DMA,
            pltpu.SemaphoreType.REGULAR,
        ],
        compiler_params=pltpu.CompilerParams(
            collective_id=0, has_side_effects=True, vmem_limit_bytes=50 << 20
        ),
        name="ladder",
    )(
        *(
            pltpu.with_memory_space_constraint(x, pltpu.HBM)
            for x in (block_sizes, amplitudes, integrals)
        )
    )
    return rows.transpose(1, 0, 2)


def solution(mesh):
    placed = (P("ab", None, None, "cd"), P(None, "ab", "cd"), P())
    return jax.shard_map(
        on_device, mesh=mesh, in_specs=placed, out_specs=P(None, "ab", None), check_vma=False
    )
```

```python
import jax
import jax.numpy as jnp
from jax import lax
from jax.experimental import pallas as pl
from jax.experimental.pallas import tpu as pltpu
from jax.sharding import PartitionSpec as P

IRREPS = 4
BLK = 128
NPAIR = 16
WIR = 24
GROUP = 8
OWN = 3
CB = 16
MESH = pl.DeviceIdType.MESH
F32 = jnp.float32
BF16 = jnp.bfloat16


def iota(shape, dim):
    return lax.broadcasted_iota(jnp.int32, shape, dim)


def split2(x, axis):
    high = x.astype(BF16)
    low = (x - high.astype(F32)).astype(BF16)
    return jnp.concatenate([high, low], axis=axis)


def kernel(
    sizes_at, amps, integrals, out, sizes, ints, plain, panels, acc, given, taken, msgs, mirror, own, halves,
    spread_pairs, keep_rows, gather_rows, take_lanes, put_rows, keep_lanes,
    sizes_sem, ints_sem, plain_sem, send_sem, item_recv, pass_send, pass_recv,
    msg_send, msg_recv, own_send, own_recv, half_send, half_recv, token,
):
    ab = lax.axis_index("ab")
    cd = lax.axis_index("cd")
    irrep = ab // GROUP
    slot = lax.rem(ab, GROUP)
    slot_low = lax.rem(slot // 2, 2)
    slot_lane = lax.rem(slot, 2)
    ring = slot // 2
    pick = slot_lane
    core = lax.rem(cd, 2)
    high = cd // 2
    other = cd ^ 1

    fetch_own = pltpu.make_async_copy(amps, plain, plain_sem)
    fetch_own.start()
    fetch_sizes = pltpu.make_async_copy(sizes_at, sizes, sizes_sem)
    fetch_sizes.start()

    along_x = [lax.rem(irrep + d, 4) * GROUP for d in range(4)]
    along_z = [lax.rem(ring + d, 4) * 2 for d in range(4)]
    along_y = [pick, 1 - pick]

    def place(half, du, dv, dy):
        if half == 0:
            return along_x[dv] + along_z[du] + along_y[dy]
        return along_x[du] + along_z[dv] + along_y[dy]

    barrier = pltpu.get_barrier_semaphore()
    for du, dv, dy in ((1, 0, 0), (3, 0, 0), (2, 0, 0), (0, 1, 0), (0, 3, 0), (0, 2, 0), (0, 0, 1)):
        pl.semaphore_signal(
            barrier, inc=1, device_id=(place(0, du, dv, dy), cd), device_id_type=MESH
        )
    for i in range(1, 4):
        pl.semaphore_signal(barrier, inc=1, device_id=(ab, cd ^ i), device_id_type=MESH)

    fetch = pltpu.make_async_copy(integrals, ints, ints_sem)
    fetch.start()

    fetch_sizes.wait()
    row_limit = sizes[irrep] - slot * CB
    col_limit = sizes[cd]
    shape = (NPAIR * CB, BLK)
    keep = ((iota(shape, 0) & (CB - 1)) < row_limit) & (iota(shape, 1) < col_limit)
    fetch_own.wait()
    turned = jnp.where(keep, plain[...].reshape(shape).astype(F32), 0.0).T.astype(BF16)
    panels[0, ab] = turned[:, :128]
    panels[1, ab] = turned[:, 128:]

    def item_copy(i, half, peer, block):
        return pltpu.make_async_remote_copy(
            src_ref=panels.at[half, block],
            dst_ref=panels.at[half, block],
            send_sem=send_sem.at[i],
            recv_sem=item_recv.at[half, block],
            device_id=(peer, cd),
            device_id_type=MESH,
        )

    sent = []

    def send(half, block, to):
        item_copy(len(sent), half, place(half, *to), place(half, *block)).start()
        sent.append(half)

    def arrived(half, *block):
        item_copy(0, half, ab, place(half, *block)).wait_recv()

    def onward(half, du, dy):
        send(half, (du, 0, dy), (0, 1, 0))
        send(half, (du, 0, dy), (0, 3, 0))
        if dy:
            send(half, (du, 0, dy), (0, 2, 0))

    both = (0, 1)

    def first_ring(du, halves=both):
        for half in halves:
            arrived(half, du, 0, 0)
            send(half, (du, 0, 0), (0, 0, 1))
            onward(half, du, 0)

    def from_partner(du, halves=both):
        for half in halves:
            arrived(half, du, 0, 1)
            onward(half, du, 1)

    from_below = ((0, 0), (1, 0))

    def relay(du, dy, halves=both):
        dv = 3 if (du, dy) in from_below else 1
        for half in halves:
            arrived(half, du, dv, dy)
            send(half, (du, dv, dy), (0, 4 - dv, 0))

    def rest_arrived(du, dy, halves=both):
        dv = 1 if (du, dy) in from_below else 3
        for half in halves:
            arrived(half, du, dv, dy)

    def far_arrived(half, du):
        for dy in range(2):
            arrived(half, du, 2, dy)

    pl.semaphore_wait(barrier, 10)

    for du in (1, 3):
        for half in range(2):
            send(half, (0, 0, 0), (du, 0, 0))
    for half in range(2):
        onward(half, 0, 0)
    for half in range(2):
        send(half, (0, 0, 0), (0, 0, 1))
    for half in range(2):
        send(half, (0, 0, 0), (2, 0, 0))

    spread_pairs[...] = (
        (iota((512, 128), 1) & 15) == ((iota((512, 128), 0) & 255) >> 4)
    ).astype(BF16)
    lane = iota((72, 128), 1)
    lane_slot, lane_item = lane >> 6, (lane >> 4) & 3
    row_a, row_b = iota((72, 128), 0) // WIR, lax.rem(iota((72, 128), 0), WIR)
    own_row = (lane_slot == ((row_b // OWN) & 1)) & (lane_item == lax.rem(row_b, OWN))
    keep_rows[pl.ds(0, 72)] = own_row.astype(F32)
    keep_rows[pl.ds(72, 72)] = ((lane_slot == slot_lane) & (lane_item == row_a)).astype(F32)
    frm = iota((80, 144), 1)
    frm_row = lax.rem(frm, 72)
    frm_a, frm_b = frm_row // WIR, lax.rem(frm_row, WIR)
    frm_slot, frm_k = frm_b // OWN, lax.rem(frm_b, OWN)
    goal = jnp.where(
        frm < 72,
        (frm_slot >> 2) * 8 + ((frm_slot >> 1) & 1) * 4 + frm_a,
        16 + frm_slot * 8 + slot_low * 4 + frm_k,
    )
    goal = (iota((80, 144), 0) == goal).astype(BF16)
    gather_rows[...] = jnp.concatenate([goal, goal], axis=1)
    frm = iota((96, 128), 0)
    take_lanes[...] = (
        iota((96, 128), 1) == (frm // 48) * 64 + (lax.rem(frm, 48) >> 4) * 16 + (frm & 15)
    ).astype(BF16)
    for a in range(OWN):
        b = iota((64, 128), 1)
        b_row = lax.rem(b, WIR) // 6
        b_row = (b // (2 * WIR)) * 16 + (b_row >> 1) * 8 + (b_row & 1) * 4 + a
        b_here = (((b // WIR) & 1) == core) & (b < IRREPS * WIR)
        put_rows[:, pl.ds(a * 128, 128)] = (
            ((iota((64, 128), 0) & 31) == b_row) & b_here
        ).astype(BF16)
    frm = iota((96, 128), 0)
    keep_lanes[...] = ((frm >> 4) == lax.rem(iota((96, 128), 1), 6)).astype(F32)
    diagonal = (iota((8, 256), 1) & 7) == iota((8, 256), 0)
    low_half = (iota((8, 256), 1) & 15) < 8

    def tile(rel, dz):
        source = irrep ^ rel
        second = source ^ irrep ^ cd
        at = lax.rem(ring + dz, 4)
        first = source * GROUP + at * 2
        weights = jnp.concatenate(
            [panels[half, pl.ds(first, 2)].reshape(256, 128) for half in range(2)], axis=1
        )
        first_c = pl.multiple_of(at * 2 * CB, 2 * CB)
        rows = ints[:, pl.ds(second * WIR, WIR), pl.ds(first_c, 2 * CB), :]
        left = jnp.concatenate([rows[:, :, :CB], rows[:, :, CB:]], axis=3)
        left = left.reshape(OWN * WIR * CB, 256)
        term = jnp.dot(left, weights, preferred_element_type=F32)
        term = term.reshape(OWN * WIR, 2, 8, 256)
        term = jnp.where(low_half[None], term[:, 0], term[:, 1])
        if dz:
            term = acc[second] + term
        acc[second] = term

    first_ring(1)
    first_ring(3)
    from_partner(0)
    relay(0, 0)
    first_ring(2)
    from_partner(1)
    from_partner(3)
    fetch.wait()
    relay(1, 0)
    relay(3, 0)
    from_partner(2)
    for i in range(1, 4):
        pl.semaphore_signal(token, inc=1, device_id=(ab, cd ^ i), device_id_type=MESH)
    relay(2, 0)
    rest_arrived(0, 0)
    for half in range(2):
        arrived(half, 0, 1, 1)
        arrived(half, 0, 3, 1)
    for rel, dz in ((0, 0), (0, 1), (0, 3), (1, 0), (3, 0)):
        tile(rel, dz)
    for du in (1, 3):
        rest_arrived(du, 0)
        for half in range(2):
            for dv in (1, 3):
                arrived(half, du, dv, 1)
    for rel, dz in ((1, 1), (1, 3), (3, 1), (3, 3)):
        tile(rel, dz)

    to_core = lax.rem(irrep, 2)

    def pass_copy(n, peer):
        return pltpu.make_async_remote_copy(
            src_ref=given.at[n],
            dst_ref=taken.at[n],
            send_sem=pass_send.at[n],
            recv_sem=pass_recv.at[n],
            device_id=(ab, peer),
            device_id_type=MESH,
        )

    my_tile = (irrep // 2 * 2 + high) * GROUP + slot

    def msg_copy(block, to_high):
        return pltpu.make_async_remote_copy(
            src_ref=msgs.at[block],
            dst_ref=mirror.at[my_tile],
            send_sem=msg_send,
            recv_sem=msg_recv,
            device_id=(block, to_high * 2 + to_core),
            device_id_type=MESH,
        )

    def local_copy():
        return pltpu.make_async_copy(msgs.at[ab], mirror.at[my_tile], msg_recv)

    def own_copy(n, peer, sender):
        return pltpu.make_async_remote_copy(
            src_ref=own.at[sender, n],
            dst_ref=own.at[sender, n],
            send_sem=own_send.at[n],
            recv_sem=own_recv.at[n],
            device_id=(ab, peer),
            device_id_type=MESH,
        )

    def half_copy(peer, sender):
        return pltpu.make_async_remote_copy(
            src_ref=halves.at[sender],
            dst_ref=halves.at[sender],
            send_sem=half_send,
            recv_sem=half_recv,
            device_id=(ab, peer),
            device_id_type=MESH,
        )

    def ending(*rels):
        folded = [
            jnp.sum(jnp.where(diagonal[None], acc[rel ^ cd], 0.0), axis=1) for rel in rels
        ]
        values = jnp.dot(
            split2(jnp.concatenate(folded, axis=0), 1),
            spread_pairs[...],
            preferred_element_type=F32,
        )
        kept = []
        for n in range(len(rels)):
            part = values[n * 72 : (n + 1) * 72]
            kept.append(jnp.concatenate([part, part], axis=0) * keep_rows[...])
        return jnp.dot(
            gather_rows[...], split2(jnp.concatenate(kept, axis=1), 0), preferred_element_type=F32
        )

    def finish(rel, placed):
        second = rel ^ cd
        pass_copy(rel // 2, other).wait_recv()
        placed = placed + taken[rel // 2]
        msgs[pl.ds(second * GROUP, GROUP)] = placed[16:].reshape(GROUP, 8, 128)
        for dz in (2, 1, 3, 0):
            for dy in (1, 0):
                for to_high in (1 - high, high):
                    block = second * GROUP + along_z[dz] + along_y[dy]
                    if dz or dy or to_high is not high:
                        msg_copy(block, to_high).start()
                        continue
                    here = (block == ab) & (to_core == core)
                    pl.when(~here)(msg_copy(block, to_high).start)
                    pl.when(here)(local_copy().start)

        at = second // 2
        own[high, at] = placed[:16].reshape(2, 8, 128)
        own_copy(at, cd ^ 2, high).start()

    far_arrived(1, 0)
    rest_arrived(2, 0, (0,))
    for dv in (1, 3):
        arrived(0, 2, dv, 1)
    far_arrived(1, 1)
    far_arrived(1, 3)
    for rel, dz in ((1, 2), (3, 2), (0, 2)):
        tile(rel, dz)
    passed = ending(1, 3)
    for n in range(2):
        given[n] = passed[:, n * 128 : (n + 1) * 128]
        pass_copy(n, other).start()
    rest_arrived(2, 0, (1,))
    for dv in (1, 3):
        arrived(1, 2, dv, 1)
    for du in (0, 1, 3):
        far_arrived(0, du)
    for dz in (0, 1, 3):
        tile(2, dz)
    far_arrived(0, 2)
    far_arrived(1, 2)
    tile(2, 2)
    pl.semaphore_wait(token, 3)
    placed = ending(2, 0)
    finish(2, placed[:, :128])
    finish(0, placed[:, 128:])

    def sent_items(i, carry):
        item_copy(i, 0, ab, ab).wait_send()
        return carry

    lax.fori_loop(0, len(sent), sent_items, 0)
    for n in range(2):
        pass_copy(n, cd).wait_send()

    pltpu.make_async_copy(msgs, mirror, msg_recv).wait()
    mirrored = jnp.sum(mirror[...].reshape(2, 2, 2, 4, 8, 128), axis=(1, 3))
    for n in range(2):
        own_copy(n, cd, 1 - high).wait_recv()
    total = ((own[0] + own[1]) + mirrored).reshape(32, 128)
    turned = lax.dot_general(
        take_lanes[...], split2(total, 0), (((1,), (1,)), ((), ())), preferred_element_type=F32
    )
    wide = jnp.dot(turned.astype(BF16), put_rows[...], preferred_element_type=F32)
    for a in range(OWN):
        part = wide[:, a * 128 : (a + 1) * 128] * keep_lanes[...]
        halves[core, a] = jnp.sum(part.reshape(6, NPAIR, 128), axis=0)
    half_copy(other, core).start()
    for n in range(2):
        own_copy(n, cd, high).wait_send()
    half_copy(cd, 1 - core).wait_recv()
    out[...] = (halves[0] + halves[1])[:, :, : IRREPS * WIR]
    half_copy(cd, core).wait_send()
    tiles = pltpu.make_async_copy(msgs.at[pl.ds(0, 31)], mirror.at[pl.ds(0, 31)], msg_send)
    tiles.wait()

    @pl.when(to_core != core)
    def _():
        pltpu.make_async_copy(msgs.at[0], mirror.at[0], msg_send).wait()


def on_device(integrals, amplitudes, block_sizes):
    vmem = pl.BlockSpec(memory_space=pltpu.VMEM)
    rows = pl.pallas_call(
        kernel,
        out_shape=jax.ShapeDtypeStruct((OWN, NPAIR, IRREPS * WIR), F32),
        in_specs=[
            pl.BlockSpec(memory_space=pltpu.HBM),
            pl.BlockSpec(memory_space=pltpu.HBM),
            pl.BlockSpec(memory_space=pltpu.HBM),
        ],
        out_specs=vmem,
        scratch_shapes=[
            pltpu.SMEM((IRREPS,), jnp.int32),
            pltpu.VMEM(integrals.shape, BF16),
            pltpu.VMEM(amplitudes.shape, BF16),
            pltpu.VMEM((2, 32, BLK, NPAIR * CB // 2), BF16),
            pltpu.VMEM((IRREPS, OWN * WIR, 8, 256), F32),
            pltpu.VMEM((2, 80, 128), F32),
            pltpu.VMEM((2, 80, 128), F32),
            pltpu.VMEM((32, 8, 128), F32),
            pltpu.VMEM((32, 8, 128), F32),
            pltpu.VMEM((2, 2, 2, 8, 128), F32),
            pltpu.VMEM((2, OWN, NPAIR, 128), F32),
            pltpu.VMEM((512, 128), BF16),
            pltpu.VMEM((144, 128), F32),
            pltpu.VMEM((80, 288), BF16),
            pltpu.VMEM((96, 128), BF16),
            pltpu.VMEM((64, OWN * 128), BF16),
            pltpu.VMEM((96, 128), F32),
            pltpu.SemaphoreType.DMA,
            pltpu.SemaphoreType.DMA,
            pltpu.SemaphoreType.DMA,
            pltpu.SemaphoreType.DMA((62,)),
            pltpu.SemaphoreType.DMA((2, 32)),
            pltpu.SemaphoreType.DMA((2,)),
            pltpu.SemaphoreType.DMA((2,)),
            pltpu.SemaphoreType.DMA,
            pltpu.SemaphoreType.DMA,
            pltpu.SemaphoreType.DMA((2,)),
            pltpu.SemaphoreType.DMA((2,)),
            pltpu.SemaphoreType.DMA,
            pltpu.SemaphoreType.DMA,
            pltpu.SemaphoreType.REGULAR,
        ],
        compiler_params=pltpu.CompilerParams(
            collective_id=0, has_side_effects=True, vmem_limit_bytes=50 << 20
        ),
        name="ladder",
    )(
        *(
            pltpu.with_memory_space_constraint(x, pltpu.HBM)
            for x in (block_sizes, amplitudes, integrals)
        )
    )
    return rows.transpose(1, 0, 2)


def solution(mesh):
    placed = (P("ab", None, None, "cd"), P(None, "ab", "cd"), P())
    return jax.shard_map(
        on_device, mesh=mesh, in_specs=placed, out_specs=P(None, "ab", None), check_vma=False
    )
```

```python
import jax
import jax.numpy as jnp
from jax import lax
from jax.experimental import pallas as pl
from jax.experimental.pallas import tpu as pltpu
from jax.sharding import PartitionSpec as P

IRREPS = 4
BLK = 128
NPAIR = 16
WIR = 24
GROUP = 8
OWN = 3
CB = 16
MESH = pl.DeviceIdType.MESH
F32 = jnp.float32
BF16 = jnp.bfloat16


def iota(shape, dim):
    return lax.broadcasted_iota(jnp.int32, shape, dim)


def split2(x, axis):
    high = x.astype(BF16)
    low = (x - high.astype(F32)).astype(BF16)
    return jnp.concatenate([high, low], axis=axis)


def kernel(
    sizes_at, amps, integrals, out, sizes, ints, plain, panels, acc, given, taken, msgs, mirror, own, halves,
    spread_pairs, keep_rows, gather_rows, take_lanes, put_rows, keep_lanes,
    sizes_sem, ints_sem, plain_sem, send_sem, item_recv, pass_send, pass_recv,
    msg_send, msg_recv, own_send, own_recv, half_send, half_recv, token,
):
    ab = lax.axis_index("ab")
    cd = lax.axis_index("cd")
    irrep = ab // GROUP
    slot = lax.rem(ab, GROUP)
    slot_low = lax.rem(slot // 2, 2)
    slot_lane = lax.rem(slot, 2)
    ring = slot // 2
    pick = slot_lane
    core = lax.rem(cd, 2)
    high = cd // 2
    other = cd ^ 1

    fetch_own = pltpu.make_async_copy(amps, plain, plain_sem)
    fetch_own.start()
    fetch_sizes = pltpu.make_async_copy(sizes_at, sizes, sizes_sem)
    fetch_sizes.start()

    along_x = [lax.rem(irrep + d, 4) * GROUP for d in range(4)]
    along_z = [lax.rem(ring + d, 4) * 2 for d in range(4)]
    along_y = [pick, 1 - pick]

    def place(half, du, dv, dy):
        if half == 0:
            return along_x[dv] + along_z[du] + along_y[dy]
        return along_x[du] + along_z[dv] + along_y[dy]

    barrier = pltpu.get_barrier_semaphore()
    for du, dv, dy in ((2, 0, 0), (0, 2, 0), (1, 0, 0), (3, 0, 0), (0, 1, 0), (0, 3, 0), (0, 0, 1)):
        pl.semaphore_signal(
            barrier, inc=1, device_id=(place(0, du, dv, dy), cd), device_id_type=MESH
        )
    for i in range(1, 4):
        pl.semaphore_signal(barrier, inc=1, device_id=(ab, cd ^ i), device_id_type=MESH)

    fetch = pltpu.make_async_copy(integrals, ints, ints_sem)
    fetch.start()

    fetch_sizes.wait()
    row_limit = sizes[irrep] - slot * CB
    col_limit = sizes[cd]
    shape = (NPAIR * CB, BLK)
    keep = ((iota(shape, 0) & (CB - 1)) < row_limit) & (iota(shape, 1) < col_limit)
    fetch_own.wait()
    turned = jnp.where(keep, plain[...].reshape(shape).astype(F32), 0.0).T.astype(BF16)
    panels[0, ab] = turned[:, :128]
    panels[1, ab] = turned[:, 128:]

    def item_copy(i, half, peer, block):
        return pltpu.make_async_remote_copy(
            src_ref=panels.at[half, block],
            dst_ref=panels.at[half, block],
            send_sem=send_sem.at[i],
            recv_sem=item_recv.at[half, block],
            device_id=(peer, cd),
            device_id_type=MESH,
        )

    sent = []

    def send(half, block, to):
        item_copy(len(sent), half, place(half, *to), place(half, *block)).start()
        sent.append(half)

    def arrived(half, *block):
        item_copy(0, half, ab, place(half, *block)).wait_recv()

    def onward(half, du, dy):
        send(half, (du, 0, dy), (0, 1, 0))
        send(half, (du, 0, dy), (0, 3, 0))
        if dy:
            send(half, (du, 0, dy), (0, 2, 0))

    both = (0, 1)

    def first_ring(du, halves=both):
        for half in halves:
            arrived(half, du, 0, 0)
            send(half, (du, 0, 0), (0, 0, 1))
            onward(half, du, 0)

    def from_partner(du, halves=both):
        for half in halves:
            arrived(half, du, 0, 1)
            onward(half, du, 1)

    from_below = ((0, 0), (1, 0))

    def relay(du, dy, halves=both):
        dv = 3 if (du, dy) in from_below else 1
        for half in halves:
            arrived(half, du, dv, dy)
            send(half, (du, dv, dy), (0, 4 - dv, 0))

    def rest_arrived(du, dy, halves=both):
        dv = 1 if (du, dy) in from_below else 3
        for half in halves:
            arrived(half, du, dv, dy)

    def far_arrived(half, du):
        for dy in range(2):
            arrived(half, du, 2, dy)

    pl.semaphore_wait(barrier, 10)

    for du in (1, 3):
        for half in range(2):
            send(half, (0, 0, 0), (du, 0, 0))
    for half in range(2):
        onward(half, 0, 0)
    for half in range(2):
        send(half, (0, 0, 0), (0, 0, 1))
    for half in range(2):
        send(half, (0, 0, 0), (2, 0, 0))

    spread_pairs[...] = (
        (iota((512, 128), 1) & 15) == ((iota((512, 128), 0) & 255) >> 4)
    ).astype(BF16)
    lane = iota((72, 128), 1)
    lane_slot, lane_item = lane >> 6, (lane >> 4) & 3
    row_a, row_b = iota((72, 128), 0) // WIR, lax.rem(iota((72, 128), 0), WIR)
    own_row = (lane_slot == ((row_b // OWN) & 1)) & (lane_item == lax.rem(row_b, OWN))
    keep_rows[pl.ds(0, 72)] = own_row.astype(F32)
    keep_rows[pl.ds(72, 72)] = ((lane_slot == slot_lane) & (lane_item == row_a)).astype(F32)
    frm = iota((80, 144), 1)
    frm_row = lax.rem(frm, 72)
    frm_a, frm_b = frm_row // WIR, lax.rem(frm_row, WIR)
    frm_slot, frm_k = frm_b // OWN, lax.rem(frm_b, OWN)
    goal = jnp.where(
        frm < 72,
        (frm_slot >> 2) * 8 + ((frm_slot >> 1) & 1) * 4 + frm_a,
        16 + frm_slot * 8 + slot_low * 4 + frm_k,
    )
    goal = (iota((80, 144), 0) == goal).astype(BF16)
    gather_rows[...] = jnp.concatenate([goal, goal], axis=1)
    frm = iota((96, 128), 0)
    take_lanes[...] = (
        iota((96, 128), 1) == (frm // 48) * 64 + (lax.rem(frm, 48) >> 4) * 16 + (frm & 15)
    ).astype(BF16)
    for a in range(OWN):
        b = iota((64, 128), 1)
        b_row = lax.rem(b, WIR) // 6
        b_row = (b // (2 * WIR)) * 16 + (b_row >> 1) * 8 + (b_row & 1) * 4 + a
        b_here = (((b // WIR) & 1) == core) & (b < IRREPS * WIR)
        put_rows[:, pl.ds(a * 128, 128)] = (
            ((iota((64, 128), 0) & 31) == b_row) & b_here
        ).astype(BF16)
    frm = iota((96, 128), 0)
    keep_lanes[...] = ((frm >> 4) == lax.rem(iota((96, 128), 1), 6)).astype(F32)
    diagonal = (iota((8, 256), 1) & 7) == iota((8, 256), 0)
    low_half = (iota((8, 256), 1) & 15) < 8

    def tile(rel, dz):
        source = irrep ^ rel
        second = source ^ irrep ^ cd
        at = lax.rem(ring + dz, 4)
        first = source * GROUP + at * 2
        weights = jnp.concatenate(
            [panels[half, pl.ds(first, 2)].reshape(256, 128) for half in range(2)], axis=1
        )
        first_c = pl.multiple_of(at * 2 * CB, 2 * CB)
        rows = ints[:, pl.ds(second * WIR, WIR), pl.ds(first_c, 2 * CB), :]
        left = jnp.concatenate([rows[:, :, :CB], rows[:, :, CB:]], axis=3)
        left = left.reshape(OWN * WIR * CB, 256)
        term = jnp.dot(left, weights, preferred_element_type=F32)
        term = term.reshape(OWN * WIR, 2, 8, 256)
        term = jnp.where(low_half[None], term[:, 0], term[:, 1])
        if dz:
            term = acc[second] + term
        acc[second] = term

    first_ring(1)
    first_ring(3)
    from_partner(0)
    relay(0, 0)
    first_ring(2)
    from_partner(1)
    from_partner(3)
    fetch.wait()
    relay(1, 0)
    relay(3, 0)
    from_partner(2)
    for i in range(1, 4):
        pl.semaphore_signal(token, inc=1, device_id=(ab, cd ^ i), device_id_type=MESH)
    relay(2, 0)
    rest_arrived(0, 0)
    for half in range(2):
        arrived(half, 0, 1, 1)
        arrived(half, 0, 3, 1)
    for rel, dz in ((0, 0), (0, 1), (0, 3), (1, 0), (3, 0)):
        tile(rel, dz)
    for du in (1, 3):
        rest_arrived(du, 0)
        for half in range(2):
            for dv in (1, 3):
                arrived(half, du, dv, 1)
    for rel, dz in ((1, 1), (1, 3), (3, 1), (3, 3)):
        tile(rel, dz)

    to_core = lax.rem(irrep, 2)

    def pass_copy(n, peer):
        return pltpu.make_async_remote_copy(
            src_ref=given.at[n],
            dst_ref=taken.at[n],
            send_sem=pass_send.at[n],
            recv_sem=pass_recv.at[n],
            device_id=(ab, peer),
            device_id_type=MESH,
        )

    my_tile = (irrep // 2 * 2 + high) * GROUP + slot

    def msg_copy(block, to_high):
        return pltpu.make_async_remote_copy(
            src_ref=msgs.at[block],
            dst_ref=mirror.at[my_tile],
            send_sem=msg_send,
            recv_sem=msg_recv,
            device_id=(block, to_high * 2 + to_core),
            device_id_type=MESH,
        )

    def local_copy():
        return pltpu.make_async_copy(msgs.at[ab], mirror.at[my_tile], msg_recv)

    def own_copy(n, peer, sender):
        return pltpu.make_async_remote_copy(
            src_ref=own.at[sender, n],
            dst_ref=own.at[sender, n],
            send_sem=own_send.at[n],
            recv_sem=own_recv.at[n],
            device_id=(ab, peer),
            device_id_type=MESH,
        )

    def half_copy(peer, sender):
        return pltpu.make_async_remote_copy(
            src_ref=halves.at[sender],
            dst_ref=halves.at[sender],
            send_sem=half_send,
            recv_sem=half_recv,
            device_id=(ab, peer),
            device_id_type=MESH,
        )

    def ending(*rels):
        folded = [
            jnp.sum(jnp.where(diagonal[None], acc[rel ^ cd], 0.0), axis=1) for rel in rels
        ]
        values = jnp.dot(
            split2(jnp.concatenate(folded, axis=0), 1),
            spread_pairs[...],
            preferred_element_type=F32,
        )
        kept = []
        for n in range(len(rels)):
            part = values[n * 72 : (n + 1) * 72]
            kept.append(jnp.concatenate([part, part], axis=0) * keep_rows[...])
        return jnp.dot(
            gather_rows[...], split2(jnp.concatenate(kept, axis=1), 0), preferred_element_type=F32
        )

    def finish(rel, placed):
        second = rel ^ cd
        pass_copy(rel // 2, other).wait_recv()
        placed = placed + taken[rel // 2]
        at = second // 2
        own[high, at] = placed[:16].reshape(2, 8, 128)
        own_copy(at, cd ^ 2, high).start()
        msgs[pl.ds(second * GROUP, GROUP)] = placed[16:].reshape(GROUP, 8, 128)
        for dz in (2, 1, 3, 0):
            for dy in (1, 0):
                for to_high in (1 - high, high):
                    block = second * GROUP + along_z[dz] + along_y[dy]
                    if dz or dy or to_high is not high:
                        msg_copy(block, to_high).start()
                        continue
                    here = (block == ab) & (to_core == core)
                    pl.when(~here)(msg_copy(block, to_high).start)
                    pl.when(here)(local_copy().start)


    far_arrived(1, 0)
    rest_arrived(2, 0, (0,))
    for dv in (1, 3):
        arrived(0, 2, dv, 1)
    far_arrived(1, 1)
    far_arrived(1, 3)
    for rel, dz in ((1, 2), (3, 2)):
        tile(rel, dz)
    passed = ending(1, 3)
    for n in range(2):
        given[n] = passed[:, n * 128 : (n + 1) * 128]
        pass_copy(n, other).start()
    rest_arrived(2, 0, (1,))
    for dv in (1, 3):
        arrived(1, 2, dv, 1)
    for du in (0, 1, 3):
        far_arrived(0, du)
    tile(0, 2)
    for dz in (0, 1, 3):
        tile(2, dz)
    far_arrived(0, 2)
    far_arrived(1, 2)
    tile(2, 2)
    pl.semaphore_wait(token, 3)
    placed = ending(2, 0)
    finish(2, placed[:, :128])
    finish(0, placed[:, 128:])

    def sent_items(i, carry):
        item_copy(i, 0, ab, ab).wait_send()
        return carry

    lax.fori_loop(0, len(sent), sent_items, 0)
    for n in range(2):
        pass_copy(n, cd).wait_send()

    pltpu.make_async_copy(msgs, mirror, msg_recv).wait()
    mirrored = jnp.sum(mirror[...].reshape(2, 2, 2, 4, 8, 128), axis=(1, 3))
    for n in range(2):
        own_copy(n, cd, 1 - high).wait_recv()
    total = ((own[0] + own[1]) + mirrored).reshape(32, 128)
    turned = lax.dot_general(
        take_lanes[...], split2(total, 0), (((1,), (1,)), ((), ())), preferred_element_type=F32
    )
    wide = jnp.dot(turned.astype(BF16), put_rows[...], preferred_element_type=F32)
    for a in range(OWN):
        part = wide[:, a * 128 : (a + 1) * 128] * keep_lanes[...]
        halves[core, a] = jnp.sum(part.reshape(6, NPAIR, 128), axis=0)
    half_copy(other, core).start()
    for n in range(2):
        own_copy(n, cd, high).wait_send()
    tiles = pltpu.make_async_copy(msgs.at[pl.ds(0, 31)], mirror.at[pl.ds(0, 31)], msg_send)
    tiles.wait()

    @pl.when(to_core != core)
    def _():
        pltpu.make_async_copy(msgs.at[0], mirror.at[0], msg_send).wait()

    half_copy(cd, 1 - core).wait_recv()
    out[...] = (halves[0] + halves[1])[:, :, : IRREPS * WIR]
    half_copy(cd, core).wait_send()


def on_device(integrals, amplitudes, block_sizes):
    vmem = pl.BlockSpec(memory_space=pltpu.VMEM)
    rows = pl.pallas_call(
        kernel,
        out_shape=jax.ShapeDtypeStruct((OWN, NPAIR, IRREPS * WIR), F32),
        in_specs=[
            pl.BlockSpec(memory_space=pltpu.HBM),
            pl.BlockSpec(memory_space=pltpu.HBM),
            pl.BlockSpec(memory_space=pltpu.HBM),
        ],
        out_specs=vmem,
        scratch_shapes=[
            pltpu.SMEM((IRREPS,), jnp.int32),
            pltpu.VMEM(integrals.shape, BF16),
            pltpu.VMEM(amplitudes.shape, BF16),
            pltpu.VMEM((2, 32, BLK, NPAIR * CB // 2), BF16),
            pltpu.VMEM((IRREPS, OWN * WIR, 8, 256), F32),
            pltpu.VMEM((2, 80, 128), F32),
            pltpu.VMEM((2, 80, 128), F32),
            pltpu.VMEM((32, 8, 128), F32),
            pltpu.VMEM((32, 8, 128), F32),
            pltpu.VMEM((2, 2, 2, 8, 128), F32),
            pltpu.VMEM((2, OWN, NPAIR, 128), F32),
            pltpu.VMEM((512, 128), BF16),
            pltpu.VMEM((144, 128), F32),
            pltpu.VMEM((80, 288), BF16),
            pltpu.VMEM((96, 128), BF16),
            pltpu.VMEM((64, OWN * 128), BF16),
            pltpu.VMEM((96, 128), F32),
            pltpu.SemaphoreType.DMA,
            pltpu.SemaphoreType.DMA,
            pltpu.SemaphoreType.DMA,
            pltpu.SemaphoreType.DMA((62,)),
            pltpu.SemaphoreType.DMA((2, 32)),
            pltpu.SemaphoreType.DMA((2,)),
            pltpu.SemaphoreType.DMA((2,)),
            pltpu.SemaphoreType.DMA,
            pltpu.SemaphoreType.DMA,
            pltpu.SemaphoreType.DMA((2,)),
            pltpu.SemaphoreType.DMA((2,)),
            pltpu.SemaphoreType.DMA,
            pltpu.SemaphoreType.DMA,
            pltpu.SemaphoreType.REGULAR,
        ],
        compiler_params=pltpu.CompilerParams(
            collective_id=0, has_side_effects=True, vmem_limit_bytes=50 << 20
        ),
        name="ladder",
    )(
        *(
            pltpu.with_memory_space_constraint(x, pltpu.HBM)
            for x in (block_sizes, amplitudes, integrals)
        )
    )
    return rows.transpose(1, 0, 2)


def solution(mesh):
    placed = (P("ab", None, None, "cd"), P(None, "ab", "cd"), P())
    return jax.shard_map(
        on_device, mesh=mesh, in_specs=placed, out_specs=P(None, "ab", None), check_vma=False
    )
```

```python
import jax
import jax.numpy as jnp
from jax import lax
from jax.experimental import pallas as pl
from jax.experimental.pallas import tpu as pltpu
from jax.sharding import PartitionSpec as P

IRREPS = 4
BLK = 128
NPAIR = 16
WIR = 24
GROUP = 8
OWN = 3
CB = 16
MESH = pl.DeviceIdType.MESH
F32 = jnp.float32
BF16 = jnp.bfloat16


def iota(shape, dim):
    return lax.broadcasted_iota(jnp.int32, shape, dim)


def split2(x, axis):
    high = x.astype(BF16)
    low = (x - high.astype(F32)).astype(BF16)
    return jnp.concatenate([high, low], axis=axis)


def kernel(
    sizes_at, amps, integrals, out, sizes, ints, plain, panels, acc, given, taken, msgs, mirror, own, halves,
    spread_pairs, keep_rows, gather_rows, take_lanes, put_rows, keep_lanes,
    sizes_sem, ints_sem, plain_sem, send_sem, item_recv, pass_send, pass_recv,
    msg_send, msg_recv, own_send, own_recv, half_send, half_recv, token,
):
    ab = lax.axis_index("ab")
    cd = lax.axis_index("cd")
    irrep = ab // GROUP
    slot = lax.rem(ab, GROUP)
    slot_low = lax.rem(slot // 2, 2)
    slot_lane = lax.rem(slot, 2)
    ring = slot // 2
    pick = slot_lane
    core = lax.rem(cd, 2)
    high = cd // 2
    other = cd ^ 1

    fetch_own = pltpu.make_async_copy(amps, plain, plain_sem)
    fetch_own.start()
    fetch_sizes = pltpu.make_async_copy(sizes_at, sizes, sizes_sem)
    fetch_sizes.start()

    along_x = [lax.rem(irrep + d, 4) * GROUP for d in range(4)]
    along_z = [lax.rem(ring + d, 4) * 2 for d in range(4)]
    along_y = [pick, 1 - pick]

    def place(half, du, dv, dy):
        if half == 0:
            return along_x[dv] + along_z[du] + along_y[dy]
        return along_x[du] + along_z[dv] + along_y[dy]

    barrier = pltpu.get_barrier_semaphore()
    for du, dv, dy in ((2, 0, 0), (0, 2, 0), (1, 0, 0), (3, 0, 0), (0, 1, 0), (0, 3, 0), (0, 0, 1)):
        pl.semaphore_signal(
            barrier, inc=1, device_id=(place(0, du, dv, dy), cd), device_id_type=MESH
        )
    for i in range(1, 4):
        pl.semaphore_signal(barrier, inc=1, device_id=(ab, cd ^ i), device_id_type=MESH)

    fetch = pltpu.make_async_copy(integrals, ints, ints_sem)
    fetch.start()

    fetch_sizes.wait()
    row_limit = sizes[irrep] - slot * CB
    col_limit = sizes[cd]
    shape = (NPAIR * CB, BLK)
    keep = ((iota(shape, 0) & (CB - 1)) < row_limit) & (iota(shape, 1) < col_limit)
    fetch_own.wait()
    turned = jnp.where(keep, plain[...].reshape(shape).astype(F32), 0.0).T.astype(BF16)
    panels[0, ab] = turned[:, :128]
    panels[1, ab] = turned[:, 128:]

    def item_copy(i, half, peer, block):
        return pltpu.make_async_remote_copy(
            src_ref=panels.at[half, block],
            dst_ref=panels.at[half, block],
            send_sem=send_sem.at[i],
            recv_sem=item_recv.at[half, block],
            device_id=(peer, cd),
            device_id_type=MESH,
        )

    sent = []

    def send(half, block, to):
        item_copy(len(sent), half, place(half, *to), place(half, *block)).start()
        sent.append(half)

    def arrived(half, *block):
        item_copy(0, half, ab, place(half, *block)).wait_recv()

    def onward(half, du, dy):
        send(half, (du, 0, dy), (0, 1, 0))
        send(half, (du, 0, dy), (0, 3, 0))
        if dy:
            send(half, (du, 0, dy), (0, 2, 0))

    both = (0, 1)

    def first_ring(du, halves=both):
        for half in halves:
            arrived(half, du, 0, 0)
            send(half, (du, 0, 0), (0, 0, 1))
            onward(half, du, 0)

    def from_partner(du, halves=both):
        for half in halves:
            arrived(half, du, 0, 1)
            onward(half, du, 1)

    from_below = ((0, 0), (1, 0))

    def relay(du, dy, halves=both):
        dv = 3 if (du, dy) in from_below else 1
        for half in halves:
            arrived(half, du, dv, dy)
            send(half, (du, dv, dy), (0, 4 - dv, 0))

    def rest_arrived(du, dy, halves=both):
        dv = 1 if (du, dy) in from_below else 3
        for half in halves:
            arrived(half, du, dv, dy)

    def far_arrived(half, du):
        for dy in range(2):
            arrived(half, du, 2, dy)

    pl.semaphore_wait(barrier, 10)

    for du in (1, 3):
        for half in range(2):
            send(half, (0, 0, 0), (du, 0, 0))
    for half in range(2):
        onward(half, 0, 0)
    for half in range(2):
        send(half, (0, 0, 0), (0, 0, 1))
    for half in range(2):
        send(half, (0, 0, 0), (2, 0, 0))

    spread_pairs[...] = (
        (iota((512, 128), 1) & 15) == ((iota((512, 128), 0) & 255) >> 4)
    ).astype(BF16)
    lane = iota((72, 128), 1)
    lane_slot, lane_item = lane >> 6, (lane >> 4) & 3
    row_a, row_b = iota((72, 128), 0) // WIR, lax.rem(iota((72, 128), 0), WIR)
    own_row = (lane_slot == ((row_b // OWN) & 1)) & (lane_item == lax.rem(row_b, OWN))
    keep_rows[pl.ds(0, 72)] = own_row.astype(F32)
    keep_rows[pl.ds(72, 72)] = ((lane_slot == slot_lane) & (lane_item == row_a)).astype(F32)
    frm = iota((80, 144), 1)
    frm_row = lax.rem(frm, 72)
    frm_a, frm_b = frm_row // WIR, lax.rem(frm_row, WIR)
    frm_slot, frm_k = frm_b // OWN, lax.rem(frm_b, OWN)
    goal = jnp.where(
        frm < 72,
        (frm_slot >> 2) * 8 + ((frm_slot >> 1) & 1) * 4 + frm_a,
        16 + frm_slot * 8 + slot_low * 4 + frm_k,
    )
    goal = (iota((80, 144), 0) == goal).astype(BF16)
    gather_rows[...] = jnp.concatenate([goal, goal], axis=1)
    frm = iota((96, 128), 0)
    take_lanes[...] = (
        iota((96, 128), 1) == (frm // 48) * 64 + (lax.rem(frm, 48) >> 4) * 16 + (frm & 15)
    ).astype(BF16)
    for a in range(OWN):
        b = iota((64, 128), 1)
        b_row = lax.rem(b, WIR) // 6
        b_row = (b // (2 * WIR)) * 16 + (b_row >> 1) * 8 + (b_row & 1) * 4 + a
        b_here = (((b // WIR) & 1) == core) & (b < IRREPS * WIR)
        put_rows[:, pl.ds(a * 128, 128)] = (
            ((iota((64, 128), 0) & 31) == b_row) & b_here
        ).astype(BF16)
    frm = iota((96, 128), 0)
    keep_lanes[...] = ((frm >> 4) == lax.rem(iota((96, 128), 1), 6)).astype(F32)
    diagonal = (iota((8, 256), 1) & 7) == iota((8, 256), 0)
    low_half = (iota((8, 256), 1) & 15) < 8

    def tile(rel, dz):
        source = irrep ^ rel
        second = source ^ irrep ^ cd
        at = lax.rem(ring + dz, 4)
        first = source * GROUP + at * 2
        weights = jnp.concatenate(
            [panels[half, pl.ds(first, 2)].reshape(256, 128) for half in range(2)], axis=1
        )
        first_c = pl.multiple_of(at * 2 * CB, 2 * CB)
        rows = ints[:, pl.ds(second * WIR, WIR), pl.ds(first_c, 2 * CB), :]
        left = jnp.concatenate([rows[:, :, :CB], rows[:, :, CB:]], axis=3)
        left = left.reshape(OWN * WIR * CB, 256)
        term = jnp.dot(left, weights, preferred_element_type=F32)
        term = term.reshape(OWN * WIR, 2, 8, 256)
        term = jnp.where(low_half[None], term[:, 0], term[:, 1])
        if dz:
            term = acc[second] + term
        acc[second] = term

    first_ring(1)
    first_ring(3)
    from_partner(0)
    relay(0, 0)
    first_ring(2)
    from_partner(1)
    from_partner(3)
    fetch.wait()
    relay(1, 0)
    relay(3, 0)
    from_partner(2)
    for i in range(1, 4):
        pl.semaphore_signal(token, inc=1, device_id=(ab, cd ^ i), device_id_type=MESH)
    rest_arrived(0, 0)
    for half in range(2):
        arrived(half, 0, 1, 1)
        arrived(half, 0, 3, 1)
    for rel, dz in ((0, 0), (0, 1), (0, 3), (1, 0), (3, 0)):
        tile(rel, dz)
    relay(2, 0)
    for du in (1, 3):
        rest_arrived(du, 0)
        for half in range(2):
            for dv in (1, 3):
                arrived(half, du, dv, 1)
    for rel, dz in ((1, 1), (1, 3), (3, 1), (3, 3)):
        tile(rel, dz)

    to_core = lax.rem(irrep, 2)

    def pass_copy(n, peer):
        return pltpu.make_async_remote_copy(
            src_ref=given.at[n],
            dst_ref=taken.at[n],
            send_sem=pass_send.at[n],
            recv_sem=pass_recv.at[n],
            device_id=(ab, peer),
            device_id_type=MESH,
        )

    my_tile = (irrep // 2 * 2 + high) * GROUP + slot

    def msg_copy(block, to_high):
        return pltpu.make_async_remote_copy(
            src_ref=msgs.at[block],
            dst_ref=mirror.at[my_tile],
            send_sem=msg_send,
            recv_sem=msg_recv,
            device_id=(block, to_high * 2 + to_core),
            device_id_type=MESH,
        )

    def local_copy():
        return pltpu.make_async_copy(msgs.at[ab], mirror.at[my_tile], msg_recv)

    def own_copy(n, peer, sender):
        return pltpu.make_async_remote_copy(
            src_ref=own.at[sender, n],
            dst_ref=own.at[sender, n],
            send_sem=own_send.at[n],
            recv_sem=own_recv.at[n],
            device_id=(ab, peer),
            device_id_type=MESH,
        )

    def half_copy(peer, sender):
        return pltpu.make_async_remote_copy(
            src_ref=halves.at[sender],
            dst_ref=halves.at[sender],
            send_sem=half_send,
            recv_sem=half_recv,
            device_id=(ab, peer),
            device_id_type=MESH,
        )

    def ending(*rels):
        folded = [
            jnp.sum(jnp.where(diagonal[None], acc[rel ^ cd], 0.0), axis=1) for rel in rels
        ]
        values = jnp.dot(
            split2(jnp.concatenate(folded, axis=0), 1),
            spread_pairs[...],
            preferred_element_type=F32,
        )
        kept = []
        for n in range(len(rels)):
            part = values[n * 72 : (n + 1) * 72]
            kept.append(jnp.concatenate([part, part], axis=0) * keep_rows[...])
        return jnp.dot(
            gather_rows[...], split2(jnp.concatenate(kept, axis=1), 0), preferred_element_type=F32
        )

    def finish(rel, placed):
        second = rel ^ cd
        pass_copy(rel // 2, other).wait_recv()
        placed = placed + taken[rel // 2]
        at = second // 2
        own[high, at] = placed[:16].reshape(2, 8, 128)
        own_copy(at, cd ^ 2, high).start()
        msgs[pl.ds(second * GROUP, GROUP)] = placed[16:].reshape(GROUP, 8, 128)
        for dz in (2, 1, 3, 0):
            for dy in (1, 0):
                for to_high in (1 - high, high):
                    block = second * GROUP + along_z[dz] + along_y[dy]
                    if dz or dy or to_high is not high:
                        msg_copy(block, to_high).start()
                        continue
                    here = (block == ab) & (to_core == core)
                    pl.when(~here)(msg_copy(block, to_high).start)
                    pl.when(here)(local_copy().start)


    far_arrived(1, 0)
    rest_arrived(2, 0, (0,))
    for dv in (1, 3):
        arrived(0, 2, dv, 1)
    far_arrived(1, 1)
    far_arrived(1, 3)
    for rel, dz in ((1, 2), (3, 2)):
        tile(rel, dz)
    passed = ending(1, 3)
    for n in range(2):
        given[n] = passed[:, n * 128 : (n + 1) * 128]
        pass_copy(n, other).start()
    rest_arrived(2, 0, (1,))
    for dv in (1, 3):
        arrived(1, 2, dv, 1)
    for du in (0, 1, 3):
        far_arrived(0, du)
    tile(0, 2)
    for dz in (0, 1, 3):
        tile(2, dz)
    far_arrived(0, 2)
    far_arrived(1, 2)
    tile(2, 2)
    pl.semaphore_wait(token, 3)
    placed = ending(2, 0)
    finish(2, placed[:, :128])
    finish(0, placed[:, 128:])

    def sent_items(i, carry):
        item_copy(i, 0, ab, ab).wait_send()
        return carry

    lax.fori_loop(0, len(sent), sent_items, 0)
    for n in range(2):
        pass_copy(n, cd).wait_send()

    pltpu.make_async_copy(msgs, mirror, msg_recv).wait()
    mirrored = jnp.sum(mirror[...].reshape(2, 2, 2, 4, 8, 128), axis=(1, 3))
    for n in range(2):
        own_copy(n, cd, 1 - high).wait_recv()
    total = ((own[0] + own[1]) + mirrored).reshape(32, 128)
    turned = lax.dot_general(
        take_lanes[...], split2(total, 0), (((1,), (1,)), ((), ())), preferred_element_type=F32
    )
    wide = jnp.dot(turned.astype(BF16), put_rows[...], preferred_element_type=F32)
    for a in range(OWN):
        part = wide[:, a * 128 : (a + 1) * 128] * keep_lanes[...]
        halves[core, a] = jnp.sum(part.reshape(6, NPAIR, 128), axis=0)
    half_copy(other, core).start()
    for n in range(2):
        own_copy(n, cd, high).wait_send()
    tiles = pltpu.make_async_copy(msgs.at[pl.ds(0, 31)], mirror.at[pl.ds(0, 31)], msg_send)
    tiles.wait()

    @pl.when(to_core != core)
    def _():
        pltpu.make_async_copy(msgs.at[0], mirror.at[0], msg_send).wait()

    half_copy(cd, 1 - core).wait_recv()
    out[...] = (halves[0] + halves[1])[:, :, : IRREPS * WIR]
    half_copy(cd, core).wait_send()


def on_device(integrals, amplitudes, block_sizes):
    vmem = pl.BlockSpec(memory_space=pltpu.VMEM)
    rows = pl.pallas_call(
        kernel,
        out_shape=jax.ShapeDtypeStruct((OWN, NPAIR, IRREPS * WIR), F32),
        in_specs=[
            pl.BlockSpec(memory_space=pltpu.HBM),
            pl.BlockSpec(memory_space=pltpu.HBM),
            pl.BlockSpec(memory_space=pltpu.HBM),
        ],
        out_specs=vmem,
        scratch_shapes=[
            pltpu.SMEM((IRREPS,), jnp.int32),
            pltpu.VMEM(integrals.shape, BF16),
            pltpu.VMEM(amplitudes.shape, BF16),
            pltpu.VMEM((2, 32, BLK, NPAIR * CB // 2), BF16),
            pltpu.VMEM((IRREPS, OWN * WIR, 8, 256), F32),
            pltpu.VMEM((2, 80, 128), F32),
            pltpu.VMEM((2, 80, 128), F32),
            pltpu.VMEM((32, 8, 128), F32),
            pltpu.VMEM((32, 8, 128), F32),
            pltpu.VMEM((2, 2, 2, 8, 128), F32),
            pltpu.VMEM((2, OWN, NPAIR, 128), F32),
            pltpu.VMEM((512, 128), BF16),
            pltpu.VMEM((144, 128), F32),
            pltpu.VMEM((80, 288), BF16),
            pltpu.VMEM((96, 128), BF16),
            pltpu.VMEM((64, OWN * 128), BF16),
            pltpu.VMEM((96, 128), F32),
            pltpu.SemaphoreType.DMA,
            pltpu.SemaphoreType.DMA,
            pltpu.SemaphoreType.DMA,
            pltpu.SemaphoreType.DMA((62,)),
            pltpu.SemaphoreType.DMA((2, 32)),
            pltpu.SemaphoreType.DMA((2,)),
            pltpu.SemaphoreType.DMA((2,)),
            pltpu.SemaphoreType.DMA,
            pltpu.SemaphoreType.DMA,
            pltpu.SemaphoreType.DMA((2,)),
            pltpu.SemaphoreType.DMA((2,)),
            pltpu.SemaphoreType.DMA,
            pltpu.SemaphoreType.DMA,
            pltpu.SemaphoreType.REGULAR,
        ],
        compiler_params=pltpu.CompilerParams(
            collective_id=0, has_side_effects=True, vmem_limit_bytes=50 << 20
        ),
        name="ladder",
    )(
        *(
            pltpu.with_memory_space_constraint(x, pltpu.HBM)
            for x in (block_sizes, amplitudes, integrals)
        )
    )
    return rows.transpose(1, 0, 2)


def solution(mesh):
    placed = (P("ab", None, None, "cd"), P(None, "ab", "cd"), P())
    return jax.shard_map(
        on_device, mesh=mesh, in_specs=placed, out_specs=P(None, "ab", None), check_vma=False
    )
```
